256 devices in a mesh: dp: 8 (over z), tensor: 32 (over x, y, core).
Axes of the slice: x: 4, y: 4, z: 8, core: 2. Of those that a mesh axis runs over, the one named last changes fastest.
Arguments:
- tokens: bfloat16 [2048, 5120], P(('dp', 'tensor')), may hold values from -24 to 24
- gate_weight: bfloat16 [6912, 5120], P('tensor'), may hold values from -0.078125 to 0.078125
- up_weight: bfloat16 [6912, 5120], P('tensor'), may hold values from -0.078125 to 0.078125
- down_weight: bfloat16 [6912, 5120], P('tensor'), may hold values from -0.078125 to 0.078125
- residual_carry: bfloat16 [8, 32, 256, 5120], P('dp', 'tensor'), may hold values from -2.5 to 2.5
- forward_blocks: int32 [8, 32, 32, 10], P('dp', 'tensor'), may hold values from 0 to 39, as said below
- forward_counts: int32 [8, 32, 32], P('dp', 'tensor'), may hold values from 1 to 10, as said below
- cotangent: bfloat16 [2048, 5120], P(('dp', 'tensor')), may hold values from -24 to 24
- backward_blocks: int32 [8, 32, 32, 10], P('dp', 'tensor'), may hold values from 0 to 39, as said below
- backward_counts: int32 [8, 32, 32], P('dp', 'tensor'), may hold values from 1 to 10, as said below
Outputs:
- layer_output: bfloat16 [2048, 5120], P(('dp', 'tensor'))
- residual_next: bfloat16 [8, 32, 256, 5120], P('dp', 'tensor')
- input_gradient: bfloat16 [2048, 5120], P(('dp', 'tensor'))
- gate_gradient: bfloat16 [6912, 5120], P('tensor', 'dp')
- up_gradient: bfloat16 [6912, 5120], P('tensor', 'dp')
- down_gradient: bfloat16 [6912, 5120], P('tensor', 'dp')
The draws below stay inside these ranges and needn't reach their ends.
Inputs may be any that keep to these rules, and one draw needn't show every extreme that they name: `forward_blocks`: for each group, source and destination the 10 block numbers are all different. `forward_counts`: in each dp group one destination receives 10 blocks from every source. `backward_blocks`: for each group, source and destination the 10 block numbers are all different. `backward_counts`: in each dp group one destination receives 10 blocks from every source.
All inputs are finite; a program needn't handle non-finite values.
Results may differ from the reference program's by a relative error of at most 0.005.
Values may be sent and summed in bfloat16 or wider, within the bound.
No kernel may reach another device: no remote copies, remote signals or barrier semaphores. Data moves between devices by JAX's collectives and lax.ppermute only.
A program may use at most 128 MiB of HBM per device.

```python
import jax
import jax.numpy as jnp
from jax import lax

D = 5120
FF = 6912
TOK_DEV = 8
KMAX = 10
NB = 40
TOK_GRP = 256
TOKENS = 2048
N_DP = 8
N_TENSOR = 32


def block_lists(key):
    total = N_DP * N_TENSOR * N_TENSOR
    keys = jax.random.split(key, total)
    orders = jax.vmap(lambda single: jax.random.permutation(single, jnp.arange(NB, dtype=jnp.int32)))(keys)
    return orders[:, :KMAX].reshape(N_DP, N_TENSOR, N_TENSOR, KMAX).astype(jnp.int32)


def block_counts(key):
    first_key, second_key = jax.random.split(key)
    counts = jax.random.randint(first_key, (N_DP, N_TENSOR, N_TENSOR), 1, KMAX + 1)
    target = jax.random.randint(second_key, (N_DP, 1, 1), 0, N_TENSOR)
    places = jnp.arange(N_TENSOR, dtype=jnp.int32)[None, None, :]
    return jnp.where(places == target, KMAX, counts).astype(jnp.int32)


def draw_forward_blocks(key, part):
    key = jax.random.fold_in(key, 11)
    return block_lists(key)


def draw_forward_counts(key, part):
    key = jax.random.fold_in(key, 12)
    return block_counts(key)


def draw_backward_blocks(key, part):
    key = jax.random.fold_in(key, 13)
    return block_lists(key)


def draw_backward_counts(key, part):
    key = jax.random.fold_in(key, 14)
    return block_counts(key)


def spiked(array, key, source, target, shards_of, factor):
    def block_of(position):
        return (jnp.arange(array.shape[position]) // (array.shape[position] // shards_of)).reshape((-1,) + (1,) * (array.ndim - 1 - position))

    near = jax.random.permutation(key, shards_of)[block_of(target)]
    far = (block_of(target) + shards_of // 2) % shards_of
    return jnp.where((block_of(source) == near) | (block_of(source) == far), factor * array, array)


def block_levels(key, extent, cuts, smallest, high):
    loudness = 1.0
    for axis_at, shards_of in cuts:
        draws = jax.random.uniform(jax.random.fold_in(jax.random.fold_in(key, 6), axis_at), (shards_of,), jnp.float32, smallest / len(cuts), high / len(cuts))
        loudness = loudness * jnp.repeat(jnp.exp(draws), extent[axis_at] // shards_of).reshape((-1,) + (1,) * (len(extent) - 1 - axis_at))
    return loudness


def noise(stream_key, extent, spread, limit, pieces=(), kind=jnp.bfloat16):
    drawn = jax.random.normal(stream_key, extent, jnp.float32) * spread
    if len(pieces) > 0:
        drawn = block_levels(stream_key, extent, pieces, -0.22, 0.18) * drawn
    return jnp.clip(drawn, min=-limit, max=limit).astype(kind)


def noise_with(stream_key, extent, deviation, most, pieces, heavy, held_as=jnp.bfloat16):
    entries = deviation * jax.random.normal(stream_key, extent, jnp.float32)
    if pieces:
        entries = entries * block_levels(stream_key, extent, pieces, -0.22, 0.18)
    return jnp.clip(spiked(entries, jax.random.fold_in(stream_key, 3), *heavy), -most, most).astype(held_as)


def setup_inputs(seed: int = 0) -> dict:
    seeds = jax.random.split(jax.random.key(seed), 11)
    tokens = noise_with(seeds[0], (TOKENS, D), 1.0, 24.0, ((0, 256),), (0, 1, 256, 6.0))
    gate_weight = noise(seeds[1], (FF, D), D ** -0.5, 0.078125, ((0, 32),))
    up_weight = noise(seeds[2], (FF, D), D ** -0.5, 0.078125, ((0, 32),))
    down_weight = noise(seeds[3], (FF, D), FF ** -0.5, 0.078125, ((0, 32),))
    residual_carry = noise_with(seeds[4], (N_DP, N_TENSOR, TOK_GRP, D), 0.2, 2.5, ((0, 8), (1, 32)), (1, 2, 32, 2.75))
    forward_blocks = draw_forward_blocks(jax.random.fold_in(seeds[10], 71), 0)
    forward_counts = draw_forward_counts(jax.random.fold_in(seeds[10], 71), 0)
    cotangent = noise_with(seeds[7], (TOKENS, D), 1.0, 24.0, ((0, 256),), (0, 1, 256, 6.0))
    backward_blocks = draw_backward_blocks(jax.random.fold_in(seeds[10], 71), 0)
    backward_counts = draw_backward_counts(jax.random.fold_in(seeds[10], 71), 0)
    return dict(tokens=tokens, gate_weight=gate_weight, up_weight=up_weight, down_weight=down_weight, residual_carry=residual_carry, forward_blocks=forward_blocks, forward_counts=forward_counts, cotangent=cotangent, backward_blocks=backward_blocks, backward_counts=backward_counts)


def block_choice(blocks, counts):
    valid = jnp.arange(KMAX)[None, None, :] < counts[:, :, None]
    matched = (blocks[:, :, :, None] == jnp.arange(NB)[None, None, None, :]) & valid[:, :, :, None]
    return jnp.any(matched, axis=2).astype(jnp.float32)


def reference(tokens, gate_weight, up_weight, down_weight, residual_carry, forward_blocks, forward_counts, cotangent, backward_blocks, backward_counts):
    width = FF // N_TENSOR
    gate_act = jnp.dot(tokens, gate_weight.T, preferred_element_type=jnp.float32)
    up_act = jnp.dot(tokens, up_weight.T, preferred_element_type=jnp.float32)
    sigmoid_gate = jax.nn.sigmoid(gate_act)
    silu_gate = gate_act * sigmoid_gate
    hidden = (silu_gate * up_act).astype(jnp.bfloat16)
    hidden_back = jnp.dot(cotangent, down_weight.T, preferred_element_type=jnp.float32)
    up_back = (hidden_back * silu_gate).astype(jnp.bfloat16)
    gate_back = (hidden_back * up_act * (sigmoid_gate * (1.0 + gate_act * (1.0 - sigmoid_gate)))).astype(jnp.bfloat16)
    down_split = down_weight.astype(jnp.float32).reshape(N_TENSOR, width, D)
    gate_split = gate_weight.astype(jnp.float32).reshape(N_TENSOR, width, D)
    up_split = up_weight.astype(jnp.float32).reshape(N_TENSOR, width, D)

    def per_group(group_index):
        start = (group_index * TOK_GRP).astype(jnp.int32)
        hidden_rows = lax.dynamic_slice_in_dim(hidden, start, TOK_GRP, 0).astype(jnp.float32).reshape(TOK_GRP, N_TENSOR, width)
        partial_value = jnp.einsum('rsf,sfd->srd', hidden_rows, down_split)
        corrected = partial_value + residual_carry[group_index].astype(jnp.float32)
        chosen = block_choice(forward_blocks[group_index], forward_counts[group_index])[:, :, None, :, None]
        shaped = corrected.reshape(N_TENSOR, N_TENSOR, TOK_DEV, NB, 128)
        output_rows = jnp.sum(shaped * chosen, axis=0).reshape(TOK_GRP, D)
        kept = (shaped * (1.0 - chosen)).reshape(N_TENSOR, TOK_GRP, D).astype(jnp.bfloat16)
        gate_rows = lax.dynamic_slice_in_dim(gate_back, start, TOK_GRP, 0).astype(jnp.float32).reshape(TOK_GRP, N_TENSOR, width)
        up_rows = lax.dynamic_slice_in_dim(up_back, start, TOK_GRP, 0).astype(jnp.float32).reshape(TOK_GRP, N_TENSOR, width)
        input_partial = jnp.einsum('rsf,sfd->srd', gate_rows, gate_split) + jnp.einsum('rsf,sfd->srd', up_rows, up_split)
        back_chosen = block_choice(backward_blocks[group_index], backward_counts[group_index])[:, :, None, :, None]
        back_shaped = input_partial.reshape(N_TENSOR, N_TENSOR, TOK_DEV, NB, 128)
        gradient_rows = jnp.sum(back_shaped * back_chosen, axis=0).reshape(TOK_GRP, D)
        return output_rows.astype(jnp.bfloat16), kept, gradient_rows.astype(jnp.bfloat16)

    outputs, residual_next, gradients = lax.map(per_group, jnp.arange(N_DP, dtype=jnp.int32))
    layer_output = outputs.reshape(TOKENS, D)
    input_gradient = gradients.reshape(TOKENS, D)
    gate_gradient = jnp.dot(gate_back.T, tokens, preferred_element_type=jnp.float32).astype(jnp.bfloat16)
    up_gradient = jnp.dot(up_back.T, tokens, preferred_element_type=jnp.float32).astype(jnp.bfloat16)
    down_gradient = jnp.dot(hidden.T, cotangent, preferred_element_type=jnp.float32).astype(jnp.bfloat16)
    return (layer_output, residual_next, input_gradient, gate_gradient, up_gradient, down_gradient)
```

```python
import jax
import jax.numpy as jnp
from jax import lax
from jax.experimental import pallas as pl
from jax.experimental.pallas import tpu as pltpu
from jax.sharding import Mesh, PartitionSpec as P

T = ("x", "y", "core")
XY = ("x", "y")
D = 5120
F = 216
G = 256
KMAX = 10
SIDE = 128
BF = jnp.bfloat16
F32 = jnp.float32


def nt(a, b):
    return lax.dot_general(a, b, (((1,), (1,)), ((), ())), preferred_element_type=F32)


def tn(a, b):
    return lax.dot_general(a, b, (((0,), (0,)), ((), ())), preferred_element_type=F32)


def nn(a, b):
    return lax.dot_general(a, b, (((1,), (0,)), ((), ())), preferred_element_type=F32)


def acts_kernel(tok, cot, wg, wu, wd, out, ga, ua, hb):
    k = pl.program_id(0)

    @pl.when(k == 0)
    def _():
        ga[...] = jnp.zeros_like(ga)
        ua[...] = jnp.zeros_like(ua)
        hb[...] = jnp.zeros_like(hb)

    t = tok[...]
    ga[...] += nt(wg[...], t)
    ua[...] += nt(wu[...], t)
    hb[...] += nt(wd[...], cot[...])

    @pl.when(k == pl.num_programs(0) - 1)
    def _():
        g, u, b = ga[...], ua[...], hb[...]
        s = jax.nn.sigmoid(g)
        silu = g * s
        out[0] = (b * u * (s * (1.0 + g * (1.0 - s)))).astype(BF)
        out[1] = (b * silu).astype(BF)
        out[2] = (silu * u).astype(BF)


def acts(rows, wg, wu, wd):
    kb = 1024
    steps = D // kb
    wspec = pl.BlockSpec((F, kb), lambda k: (0, k))
    return pl.pallas_call(
        acts_kernel,
        grid=(steps,),
        in_specs=[
            pl.BlockSpec((G, kb), lambda k: (0, k)),
            pl.BlockSpec((G, kb), lambda k: (0, k + steps)),
            wspec,
            wspec,
            wspec,
        ],
        out_specs=pl.BlockSpec((3, F, G), lambda k: (0, 0, 0)),
        out_shape=jax.ShapeDtypeStruct((3, F, G), BF),
        scratch_shapes=[pltpu.VMEM((F, G), F32)] * 3,
        compiler_params=pltpu.CompilerParams(vmem_limit_bytes=32 << 20),
        cost_estimate=pl.CostEstimate(
            flops=6 * G * F * D, bytes_accessed=2 * (2 * G * D + 3 * F * D), transcendentals=G * F
        ),
        name="acts",
    )(rows, rows, wg, wu, wd)


def partial_kernel(fb, fc, bb, bc, act, wg, wu, wd, res, res_next, payload, sf, sb, pk):
    n = pl.program_id(0)
    nb = wg.shape[1]
    cols = pl.ds(pl.multiple_of(n * nb, nb), nb)
    sf[:, cols] = tn(act[2], wd[...]) + res[...].astype(F32)
    sb[:, cols] = tn(act[0], wg[...]) + tn(act[1], wu[...])

    @pl.when(n == pl.num_programs(0) - 1)
    def _():
        def one(t, carry):
            r = pl.ds(pl.multiple_of(t * 8, 8), 8)
            count = fc[t]
            for j in range(KMAX):
                at = pl.ds(pl.multiple_of(fb[t, j] * 128, 128), 128)
                tile = sf[r, at]
                pk[pl.ds(pl.multiple_of(t * 160 + j * 8, 8), 8), :] = tile
                sf[r, at] = jnp.where(j < count, 0.0, tile)
                ab = pl.ds(pl.multiple_of(bb[t, j] * 128, 128), 128)
                pk[pl.ds(pl.multiple_of(t * 160 + 80 + j * 8, 8), 8), :] = sb[r, ab]
            return carry

        lax.fori_loop(0, 32, one, 0)
        payload[...] = pk[...].astype(BF)
        res_next[...] = sf[...].astype(BF)


def partials(fb, fc, bb, bc, act, wg, wu, wd, res):
    nb = 1024
    wspec = pl.BlockSpec((F, nb), lambda n, *_: (0, n))
    return pl.pallas_call(
        partial_kernel,
        grid_spec=pltpu.PrefetchScalarGridSpec(
            num_scalar_prefetch=4,
            grid=(D // nb,),
            in_specs=[
                pl.BlockSpec((3, F, G), lambda n, *_: (0, 0, 0)),
                wspec,
                wspec,
                wspec,
                pl.BlockSpec((G, nb), lambda n, *_: (0, n)),
            ],
            out_specs=[
                pl.BlockSpec((G, D), lambda n, *_: (0, 0)),
                pl.BlockSpec((32 * 160, 128), lambda n, *_: (0, 0)),
            ],
            scratch_shapes=[
                pltpu.VMEM((G, D), F32),
                pltpu.VMEM((G, D), F32),
                pltpu.VMEM((32 * 160, 128), F32),
            ],
        ),
        out_shape=[
            jax.ShapeDtypeStruct((G, D), BF),
            jax.ShapeDtypeStruct((32 * 160, 128), BF),
        ],
        compiler_params=pltpu.CompilerParams(vmem_limit_bytes=48 << 20),
        cost_estimate=pl.CostEstimate(
            flops=6 * G * F * D, bytes_accessed=2 * (2 * G * D + 3 * F * D), transcendentals=0
        ),
        name="partials",
    )(fb, fc, bb, bc, act, wg, wu, wd, res)


def unpack_kernel(idx, data, of, ob, pk, af, ab):
    pk[...] = data[...].astype(F32)
    af[...] = jnp.zeros_like(af)
    ab[...] = jnp.zeros_like(ab)

    def one(t, carry):
        for j in range(KMAX):
            cf = pl.ds(pl.multiple_of(idx[t, j] * 128, 128), 128)
            cb = pl.ds(pl.multiple_of(idx[t, KMAX + j] * 128, 128), 128)
            af[:, cf] += pk[pl.ds(pl.multiple_of(t * 160 + j * 8, 8), 8), :]
            ab[:, cb] += pk[pl.ds(pl.multiple_of(t * 160 + 80 + j * 8, 8), 8), :]
        return carry

    lax.fori_loop(0, 32, one, 0)
    of[...] = af[:, :D].astype(BF)
    ob[...] = ab[:, :D].astype(BF)


def unpack(idx, data):
    whole = pl.BlockSpec(memory_space=pltpu.VMEM)
    return pl.pallas_call(
        unpack_kernel,
        in_specs=[pl.BlockSpec(memory_space=pltpu.SMEM), whole],
        out_specs=[whole, whole],
        out_shape=[jax.ShapeDtypeStruct((8, D), BF)] * 2,
        scratch_shapes=[
            pltpu.VMEM((32 * 160, 128), F32),
            pltpu.VMEM((8, D + 128), F32),
            pltpu.VMEM((8, D + 128), F32),
        ],
        compiler_params=pltpu.CompilerParams(vmem_limit_bytes=32 << 20),
        cost_estimate=pl.CostEstimate(flops=10**6, bytes_accessed=2 * 10**6, transcendentals=0),
        name="unpack",
    )(idx, data)


def grads_kernel(core, act, cm, co, og, ou, od, ag, au, ad):
    k = pl.program_id(0)

    @pl.when(k == 0)
    def _():
        ag[...] = jnp.zeros_like(ag)
        au[...] = jnp.zeros_like(au)
        ad[...] = jnp.zeros_like(ad)

    def add(tok_ref, cot_ref):
        tok = tok_ref[...].reshape(G, 640)
        cot = cot_ref[...].reshape(G, 640)
        ag[...] += nn(act[0, 0], tok)
        au[...] += nn(act[0, 1], tok)
        ad[...] += nn(act[0, 2], cot)

    @pl.when(core[0] == 0)
    def _():
        add(cm, co)

    @pl.when(core[0] != 0)
    def _():
        add(co, cm)

    @pl.when(k == pl.num_programs(0) - 1)
    def _():
        og[...] = ag[...].astype(BF)
        ou[...] = au[...].astype(BF)
        od[...] = ad[...].astype(BF)


def grads(core, act, cm, co):
    cspec = pl.BlockSpec((16, 1, 16, 640), lambda k, *_: (0, k, 0, 0))
    ospec = pl.BlockSpec((F, 640), lambda k, *_: (0, 0))
    return pl.pallas_call(
        grads_kernel,
        grid_spec=pltpu.PrefetchScalarGridSpec(
            num_scalar_prefetch=1,
            grid=(8,),
            in_specs=[pl.BlockSpec((1, 3, F, G), lambda k, *_: (k, 0, 0, 0)), cspec, cspec],
            out_specs=[ospec] * 3,
            scratch_shapes=[pltpu.VMEM((F, 640), F32)] * 3,
        ),
        out_shape=[jax.ShapeDtypeStruct((F, 640), BF)] * 3,
        compiler_params=pltpu.CompilerParams(vmem_limit_bytes=32 << 20),
        cost_estimate=pl.CostEstimate(
            flops=6 * G * F * D, bytes_accessed=8 * 10**6, transcendentals=0
        ),
        name="grads",
    )(core, act, cm, co)


def swap_core(v):
    return lax.ppermute(v, "core", [(0, 1), (1, 0)])


def shards(tok, wg, wu, wd, res, fb, fc, cot, bb, bc):
    core = lax.axis_index("core")
    me = lax.axis_index(T)
    fb, fc, bb, bc = fb[0, 0], fc[0, 0], bb[0, 0], bc[0, 0]
    slots = jnp.arange(KMAX)[None, :]
    lists = jnp.concatenate(
        [jnp.where(slots < fc[:, None], fb, 40), jnp.where(slots < bc[:, None], bb, 40)], axis=1
    )
    side = jnp.pad(lists.astype(BF).reshape(8, 80), ((0, 0), (0, SIDE - 80)))
    rows = lax.all_gather(jnp.concatenate([tok, cot, side], axis=1), T, axis=0, tiled=True)

    first = core == 0
    other = swap_core(jnp.where(first, cot, tok))
    chip = jnp.concatenate([jnp.where(first, tok, other), jnp.where(first, other, cot)], axis=0)
    chip = lax.all_to_all(chip.reshape(16, 8, 640).transpose(1, 0, 2), "dp", 0, 0, tiled=True)
    cm = lax.all_to_all(jnp.broadcast_to(chip[None], (16, 8, 16, 640)), XY, 0, 0, tiled=True)
    co = swap_core(cm)

    act = acts(rows, wg, wu, wd)
    everyone = lax.all_gather(act[None], "dp", axis=0, tiled=True)
    res_next, payload = partials(fb, fc, bb, bc, act, wg, wu, wd, res[0, 0])
    received = lax.all_to_all(payload.reshape(32, 160, 128), T, 0, 0, tiled=True)
    told = rows[:, 2 * D :].reshape(32, 8, SIDE)[:, :, :80].reshape(32, 32, 2 * KMAX)
    idx = lax.dynamic_index_in_dim(told, me, 1, keepdims=False).astype(jnp.int32)
    layer_output, input_gradient = unpack(idx, received.reshape(32 * 160, 128))
    gate_gradient, up_gradient, down_gradient = grads(
        core.astype(jnp.int32).reshape(1), everyone, cm, co
    )
    return (
        layer_output,
        res_next[None, None],
        input_gradient,
        gate_gradient,
        up_gradient,
        down_gradient,
    )


def solution(mesh):
    fine = Mesh(mesh.devices.reshape(8, 4, 4, 2), ("dp", "x", "y", "core"))
    row = P(("dp",) + T, None)
    return jax.shard_map(
        shards,
        mesh=fine,
        in_specs=(
            row,
            P(T, None),
            P(T, None),
            P(T, None),
            P("dp", T, None, None),
            P("dp", T, None, None),
            P("dp", T, None),
            row,
            P("dp", T, None, None),
            P("dp", T, None),
        ),
        out_specs=(row, P("dp", T, None, None), row, P(T, "dp"), P(T, "dp"), P(T, "dp")),
        check_vma=False,
    )
```

```python
import jax
import jax.numpy as jnp
from jax import lax
from jax.experimental import pallas as pl
from jax.experimental.pallas import tpu as pltpu
from jax.sharding import Mesh, PartitionSpec as P

T = ("x", "y", "core")
XY = ("x", "y")
D = 5120
F = 216
G = 256
KMAX = 10
MSG = 176
VMEM_LIMIT = 60 << 20
BF = jnp.bfloat16
F32 = jnp.float32


def nt(a, b):
    return lax.dot_general(a, b, (((1,), (1,)), ((), ())), preferred_element_type=F32)


def tn(a, b):
    return lax.dot_general(a, b, (((0,), (0,)), ((), ())), preferred_element_type=F32)


def nn(a, b):
    return lax.dot_general(a, b, (((1,), (0,)), ((), ())), preferred_element_type=F32)


def acts_kernel(order, tok, cot, wg, wu, wd, nat, out, ga, ua, hb):
    k = pl.program_id(0)

    @pl.when(k == 0)
    def _():
        ga[...] = jnp.zeros_like(ga)
        ua[...] = jnp.zeros_like(ua)
        hb[...] = jnp.zeros_like(hb)

    t = tok[...]
    ga[...] += nt(t, wg[...])
    ua[...] += nt(t, wu[...])
    hb[...] += nt(cot[...], wd[...])

    @pl.when(k == pl.num_programs(0) - 1)
    def _():
        g, u, b = ga[...], ua[...], hb[...]
        s = jax.nn.sigmoid(g)
        silu = g * s
        place = (lax.broadcasted_iota(jnp.int32, (G, G), 0) == order[0:1, :]).astype(BF)
        values = (b * u * (s * (1.0 + g * (1.0 - s))), b * silu, silu * u)
        for j in range(3):
            v = values[j].astype(BF)
            nat[j] = v
            out[j] = tn(v, place).astype(BF)


def acts(order, rows, wg, wu, wd):
    kb = 1280
    steps = D // kb
    wspec = pl.BlockSpec((F, kb), lambda k: (0, k))
    return pl.pallas_call(
        acts_kernel,
        grid=(steps,),
        in_specs=[
            pl.BlockSpec((8, G), lambda k: (0, 0)),
            pl.BlockSpec((G, kb), lambda k: (0, k)),
            pl.BlockSpec((G, kb), lambda k: (0, k + steps)),
            wspec,
            wspec,
            wspec,
        ],
        out_specs=[
            pl.BlockSpec((3, G, F), lambda k: (0, 0, 0)),
            pl.BlockSpec((3, F, G), lambda k: (0, 0, 0)),
        ],
        out_shape=[
            jax.ShapeDtypeStruct((3, G, F), BF),
            jax.ShapeDtypeStruct((3, F, G), BF),
        ],
        scratch_shapes=[pltpu.VMEM((G, F), F32)] * 3,
        compiler_params=pltpu.CompilerParams(vmem_limit_bytes=VMEM_LIMIT),
        cost_estimate=pl.CostEstimate(
            flops=6 * G * F * D, bytes_accessed=2 * (2 * G * D + 3 * F * D), transcendentals=G * F
        ),
        name="acts",
    )(order, rows, rows, wg, wu, wd)


def partial_kernel(
    fb, fc, bb, bc, act, side, wg, wu, wd, res, res_next, payload, sf, sb, pk
):
    n = pl.program_id(0)
    nb = wg.shape[1]
    cols = pl.ds(pl.multiple_of(n * nb, nb), nb)
    sf[:, cols] = nn(act[2], wd[...]) + res[...].astype(F32)
    sb[:, cols] = nn(act[0], wg[...]) + nn(act[1], wu[...])

    @pl.when(n == pl.num_programs(0) - 1)
    def _():
        def one(t, carry):
            r = pl.ds(pl.multiple_of(t * 8, 8), 8)
            count = fc[t]
            for j in range(KMAX):
                at = pl.ds(pl.multiple_of(fb[t, j] * 128, 128), 128)
                tile = sf[r, at]
                pk[pl.ds(pl.multiple_of(t * MSG + j * 8, 8), 8), :] = tile
                sf[r, at] = jnp.where(j < count, 0.0, tile)
                ab = pl.ds(pl.multiple_of(bb[t, j] * 128, 128), 128)
                pk[pl.ds(pl.multiple_of(t * MSG + 80 + j * 8, 8), 8), :] = sb[r, ab]
            pk[pl.ds(pl.multiple_of(t * MSG + 160, 8), 16), :] = side[t]
            return carry

        lax.fori_loop(0, 32, one, 0)
        payload[...] = pk[...].astype(BF)
        res_next[...] = sf[...].astype(BF)


def partials(fb, fc, bb, bc, act, side, wg, wu, wd, res):
    nb = 1280
    wspec = pl.BlockSpec((F, nb), lambda n, *_: (0, n))
    return pl.pallas_call(
        partial_kernel,
        grid_spec=pltpu.PrefetchScalarGridSpec(
            num_scalar_prefetch=4,
            grid=(D // nb,),
            in_specs=[
                pl.BlockSpec((3, G, F), lambda n, *_: (0, 0, 0)),
                pl.BlockSpec((32, 16, 128), lambda n, *_: (0, 0, 0)),
                wspec,
                wspec,
                wspec,
                pl.BlockSpec((G, nb), lambda n, *_: (0, n)),
            ],
            out_specs=[
                pl.BlockSpec((G, D), lambda n, *_: (0, 0)),
                pl.BlockSpec((32 * MSG, 128), lambda n, *_: (0, 0)),
            ],
            scratch_shapes=[
                pltpu.VMEM((G, D), F32),
                pltpu.VMEM((G, D), F32),
                pltpu.VMEM((32 * MSG, 128), F32),
            ],
        ),
        out_shape=[
            jax.ShapeDtypeStruct((G, D), BF),
            jax.ShapeDtypeStruct((32 * MSG, 128), BF),
        ],
        compiler_params=pltpu.CompilerParams(vmem_limit_bytes=VMEM_LIMIT),
        cost_estimate=pl.CostEstimate(
            flops=6 * G * F * D, bytes_accessed=2 * (2 * G * D + 3 * F * D), transcendentals=0
        ),
        name="partials",
    )(fb, fc, bb, bc, act, side, wg, wu, wd, res)


def unpack_kernel(idx, data, of, ob, pk, af, ab):
    pk[...] = data[...].astype(F32)
    af[...] = jnp.zeros_like(af)
    ab[...] = jnp.zeros_like(ab)

    def one(t, carry):
        for j in range(KMAX):
            cf = pl.ds(pl.multiple_of(idx[t, j] * 128, 128), 128)
            cb = pl.ds(pl.multiple_of(idx[t, KMAX + j] * 128, 128), 128)
            af[:, cf] += pk[pl.ds(pl.multiple_of(t * MSG + j * 8, 8), 8), :]
            ab[:, cb] += pk[pl.ds(pl.multiple_of(t * MSG + 80 + j * 8, 8), 8), :]
        return carry

    lax.fori_loop(0, 32, one, 0)
    of[...] = af[:, :D].astype(BF)
    ob[...] = ab[:, :D].astype(BF)


def unpack(idx, data):
    whole = pl.BlockSpec(memory_space=pltpu.VMEM)
    return pl.pallas_call(
        unpack_kernel,
        in_specs=[pl.BlockSpec(memory_space=pltpu.SMEM), whole],
        out_specs=[whole, whole],
        out_shape=[jax.ShapeDtypeStruct((8, D), BF)] * 2,
        scratch_shapes=[
            pltpu.VMEM((32 * MSG, 128), F32),
            pltpu.VMEM((8, D + 128), F32),
            pltpu.VMEM((8, D + 128), F32),
        ],
        compiler_params=pltpu.CompilerParams(vmem_limit_bytes=VMEM_LIMIT),
        cost_estimate=pl.CostEstimate(flops=10**6, bytes_accessed=2 * 10**6, transcendentals=0),
        name="unpack",
    )(idx, data)


def grads_kernel(core, *refs):
    act, mine, other = refs[0], refs[1:9], refs[9:17]
    og, ou, od = refs[17:]

    def rows(pieces, s, n0, n1):
        blocks = []
        for i in range(4):
            for j in range(4):
                if s < 4:
                    blocks.append(pieces[i][j, s, :, n0:n1])
                else:
                    blocks.append(pieces[4 + j][i, s - 4, :, n0:n1])
        return jnp.concatenate(blocks, axis=0)

    def run(tok, cot):
        for pieces, wanted in ((tok, ((0, og), (1, ou))), (cot, ((2, od),))):
            for n0, n1 in ((0, 256), (256, 512), (512, 640)):
                total = [None] * len(wanted)
                for s in range(8):
                    rhs = rows(pieces, s, n0, n1)
                    for q, (j, _) in enumerate(wanted):
                        term = nn(act[s, j], rhs)
                        total[q] = term if total[q] is None else total[q] + term
                for q, (_, out) in enumerate(wanted):
                    out[:, n0:n1] = total[q].astype(BF)

    @pl.when(core[0] == 0)
    def _():
        run(mine, other)

    @pl.when(core[0] != 0)
    def _():
        run(other, mine)


def grads(core, act, mine, other):
    whole = pl.BlockSpec(memory_space=pltpu.VMEM)
    return pl.pallas_call(
        grads_kernel,
        in_specs=[pl.BlockSpec(memory_space=pltpu.SMEM)] + [whole] * 17,
        out_specs=[whole] * 3,
        out_shape=[jax.ShapeDtypeStruct((F, 640), BF)] * 3,
        compiler_params=pltpu.CompilerParams(vmem_limit_bytes=VMEM_LIMIT),
        cost_estimate=pl.CostEstimate(
            flops=6 * G * F * D, bytes_accessed=8 * 10**6, transcendentals=0
        ),
        name="grads",
    )(core, act, *mine, *other)


def swap_core(v):
    return lax.ppermute(v, "core", [(0, 1), (1, 0)])


def shift(v, axis, size, by):
    return lax.ppermute(v, axis, [(i, (i + by) % size) for i in range(size)])


def shards(tok, wg, wu, wd, res, fb, fc, cot, bb, bc):
    core = lax.axis_index("core")
    first = core == 0
    which = core.astype(jnp.int32).reshape(1)
    fb, fc, bb, bc = fb[0, 0], fc[0, 0], bb[0, 0], bc[0, 0]

    rows = lax.all_gather(jnp.concatenate([tok, cot], axis=1), T, axis=0, tiled=True)

    other = swap_core(jnp.where(first, cot, tok))
    chip = jnp.concatenate([jnp.where(first, tok, other), jnp.where(first, other, cot)], axis=0)
    cols = lax.all_to_all(chip.reshape(16, 8, 640).transpose(1, 0, 2), "dp", 0, 0, tiled=True)
    halves = [cols[:4], cols[4:]]
    steps = [shift(halves[h], a, 4, s) for s in (2, 1, 3) for h, a in ((0, "x"), (1, "y"))]
    steps = lax.optimization_barrier(tuple(steps))
    four = [jnp.stack([halves[h], steps[2 + h], steps[h], steps[4 + h]]) for h in range(2)]
    four = lax.optimization_barrier(tuple(four))
    mine = [four[0], None, None, None, four[1], None, None, None]
    for s in (2, 1, 3):
        mine[s] = shift(four[0], "y", 4, s)
        mine[4 + s] = shift(four[1], "x", 4, s)
    rows, *mine = lax.optimization_barrier((rows, *mine))

    x, y = lax.axis_index("x"), lax.axis_index("y")
    a = jnp.arange(G)
    order = (((x - (a // 16) % 4) % 4) * 4 + (y - a // 64) % 4) * 16 + a % 16
    order = jnp.broadcast_to(order.astype(jnp.int32)[None], (8, G))
    slots = jnp.arange(KMAX)[None, :]
    lists = jnp.concatenate(
        [jnp.where(slots < fc[:, None], fb, 40), jnp.where(slots < bc[:, None], bb, 40)], axis=1
    )
    lists = jnp.broadcast_to(lists[:, None, :], (32, 16, 2 * KMAX))
    side = jnp.pad(lists, ((0, 0), (0, 0), (0, 128 - 2 * KMAX))).astype(F32)

    nat, act = acts(order, rows, wg, wu, wd)
    everyone = lax.all_gather(act[None], "dp", axis=0, tiled=True)
    res_next, payload = partials(fb, fc, bb, bc, nat, side, wg, wu, wd, res[0, 0])
    received = lax.all_to_all(payload.reshape(32, MSG, 128), T, 0, 0, tiled=True)
    res_next, *mine = lax.optimization_barrier((res_next, *mine))
    others = [swap_core(v) for v in mine]
    idx = received[:, 160, : 2 * KMAX].astype(jnp.int32)
    layer_output, input_gradient = unpack(idx, received.reshape(32 * MSG, 128))
    gate_gradient, up_gradient, down_gradient = grads(which, everyone, mine, others)
    return (
        layer_output,
        res_next[None, None],
        input_gradient,
        gate_gradient,
        up_gradient,
        down_gradient,
    )


def solution(mesh):
    fine = Mesh(mesh.devices.reshape(8, 4, 4, 2), ("dp", "x", "y", "core"))
    row = P(("dp",) + T, None)
    return jax.shard_map(
        shards,
        mesh=fine,
        in_specs=(
            row,
            P(T, None),
            P(T, None),
            P(T, None),
            P("dp", T, None, None),
            P("dp", T, None, None),
            P("dp", T, None),
            row,
            P("dp", T, None, None),
            P("dp", T, None),
        ),
        out_specs=(row, P("dp", T, None, None), row, P(T, "dp"), P(T, "dp"), P(T, "dp")),
        check_vma=False,
    )
```

```python
import jax
import jax.numpy as jnp
from jax import lax
from jax.experimental import pallas as pl
from jax.experimental.pallas import tpu as pltpu
from jax.sharding import Mesh, PartitionSpec as P

T = ("x", "y", "core")
XY = ("x", "y")
D = 5120
F = 216
G = 256
KMAX = 10
MSG = 176
VMEM_LIMIT = 56 << 20
BF = jnp.bfloat16
F32 = jnp.float32


def nt(a, b):
    return lax.dot_general(a, b, (((1,), (1,)), ((), ())), preferred_element_type=F32)


def tn(a, b):
    return lax.dot_general(a, b, (((0,), (0,)), ((), ())), preferred_element_type=F32)


def nn(a, b):
    return lax.dot_general(a, b, (((1,), (0,)), ((), ())), preferred_element_type=F32)


def acts_kernel(order, tok, cot, wg, wu, wd, nat, out, ga, ua, hb):
    k = pl.program_id(0)

    @pl.when(k == 0)
    def _():
        ga[...] = jnp.zeros_like(ga)
        ua[...] = jnp.zeros_like(ua)
        hb[...] = jnp.zeros_like(hb)

    t = tok[...]
    ga[...] += nt(t, wg[...])
    ua[...] += nt(t, wu[...])
    hb[...] += nt(cot[...], wd[...])

    @pl.when(k == pl.num_programs(0) - 1)
    def _():
        g, u, b = ga[...], ua[...], hb[...]
        s = jax.nn.sigmoid(g)
        silu = g * s
        place = (lax.broadcasted_iota(jnp.int32, (G, G), 0) == order[0:1, :]).astype(BF)
        values = (b * u * (s * (1.0 + g * (1.0 - s))), b * silu, silu * u)
        for j in range(3):
            v = values[j].astype(BF)
            nat[j] = v
            out[j] = tn(v, place).astype(BF)


def acts(order, rows, wg, wu, wd):
    kb = 2560
    steps = D // kb
    wspec = pl.BlockSpec((F, kb), lambda k: (0, k))
    return pl.pallas_call(
        acts_kernel,
        grid=(steps,),
        in_specs=[
            pl.BlockSpec((8, G), lambda k: (0, 0)),
            pl.BlockSpec((G, kb), lambda k: (0, k)),
            pl.BlockSpec((G, kb), lambda k: (0, k + steps)),
            wspec,
            wspec,
            wspec,
        ],
        out_specs=[
            pl.BlockSpec((3, G, F), lambda k: (0, 0, 0)),
            pl.BlockSpec((3, F, G), lambda k: (0, 0, 0)),
        ],
        out_shape=[
            jax.ShapeDtypeStruct((3, G, F), BF),
            jax.ShapeDtypeStruct((3, F, G), BF),
        ],
        scratch_shapes=[pltpu.VMEM((G, F), F32)] * 3,
        compiler_params=pltpu.CompilerParams(vmem_limit_bytes=VMEM_LIMIT),
        cost_estimate=pl.CostEstimate(
            flops=6 * G * F * D, bytes_accessed=2 * (2 * G * D + 3 * F * D), transcendentals=G * F
        ),
        name="acts",
    )(order, rows, rows, wg, wu, wd)


def hbm(v):
    return pltpu.with_memory_space_constraint(v, pltpu.HBM)


CHUNK = 1280
CHUNKS = D // CHUNK


def pack_kernel(fb, bb, act, side, wg, wu, wd, res, payload, *scratch):
    vg, vu, vd, vr, sf, sb, pf, pb, po, sem = scratch
    loads = []
    for n, (far, near) in enumerate(((wg, vg), (wu, vu), (wd, vd), (res, vr))):
        loads.append([])
        for k in range(CHUNKS):
            cols = pl.ds(k * CHUNK, CHUNK)
            at = sem.at[n * CHUNKS + k]
            loads[-1].append(pltpu.make_async_copy(far.at[:, cols], near.at[:, cols], at))
    for pair in (loads[:2], loads[2:]):
        for k in range(CHUNKS):
            pair[0][k].start()
            pair[1][k].start()

    def pack(blocks, source, packed):
        def one(t, carry):
            r = pl.ds(pl.multiple_of(t * 8, 8), 8)
            for j in range(KMAX):
                at = pl.ds(pl.multiple_of(blocks[t, j] * 128, 128), 128)
                packed[t, j * 8 : j * 8 + 8, :] = source[r, at]
            return carry

        lax.fori_loop(0, 32, one, 0)

    def send(i, lo, hi):
        part = pl.ds(lo, hi - lo)
        return pltpu.make_async_copy(
            po.at[:, part, :], payload.at[:, part, :], sem.at[4 * CHUNKS + i]
        )

    for k in range(CHUNKS):
        cols = pl.ds(k * CHUNK, CHUNK)
        loads[0][k].wait()
        loads[1][k].wait()
        sb[:, cols] = nn(act[0], vg[:, cols]) + nn(act[1], vu[:, cols])
    pack(bb, sb, pb)
    po[:, 80:160, :] = pb[...].astype(BF)
    po[:, 160:MSG, :] = side[...].astype(BF)
    back = send(0, 80, MSG)
    back.start()
    for k in range(CHUNKS):
        cols = pl.ds(k * CHUNK, CHUNK)
        loads[2][k].wait()
        loads[3][k].wait()
        sf[:, cols] = nn(act[2], vd[:, cols]) + vr[:, cols].astype(F32)
    pack(fb, sf, pf)
    po[:, 0:80, :] = pf[...].astype(BF)
    ahead = send(1, 0, 80)
    ahead.start()
    back.wait()
    ahead.wait()


def pack_selected(fb, bb, act, side, wg, wu, wd, res):
    whole = pl.BlockSpec(memory_space=pltpu.VMEM)
    smem = pl.BlockSpec(memory_space=pltpu.SMEM)
    anywhere = pl.BlockSpec(memory_space=pl.ANY)
    return pl.pallas_call(
        pack_kernel,
        in_specs=[smem] * 2 + [whole] * 2 + [anywhere] * 4,
        out_specs=anywhere,
        out_shape=pltpu.HBM((32, MSG, 128), BF),
        scratch_shapes=[pltpu.VMEM((F, D), BF)] * 3
        + [
            pltpu.VMEM((G, D), BF),
            pltpu.VMEM((G, D), F32),
            pltpu.VMEM((G, D), F32),
            pltpu.VMEM((32, 80, 128), F32),
            pltpu.VMEM((32, 80, 128), F32),
            pltpu.VMEM((32, MSG, 128), BF),
            pltpu.SemaphoreType.DMA((4 * CHUNKS + 2,)),
        ],
        compiler_params=pltpu.CompilerParams(vmem_limit_bytes=VMEM_LIMIT),
        cost_estimate=pl.CostEstimate(
            flops=6 * G * F * D, bytes_accessed=2 * (G * D + 3 * F * D), transcendentals=0
        ),
        name="pack_selected",
    )(fb, bb, act, side, hbm(wg), hbm(wu), hbm(wd), hbm(res))


def residual_kernel(fb, fc, act, wd, res, res_next, sf):
    n = pl.program_id(0)
    nb = wd.shape[1]
    cols = pl.ds(pl.multiple_of(n * nb, nb), nb)
    sf[:, cols] = nn(act[0], wd[...]) + res[...].astype(F32)

    @pl.when(n == pl.num_programs(0) - 1)
    def _():
        def one(t, carry):
            r = pl.ds(pl.multiple_of(t * 8, 8), 8)
            count = fc[t]
            for j in range(KMAX):
                at = pl.ds(pl.multiple_of(fb[t, j] * 128, 128), 128)
                sf[r, at] = jnp.where(j < count, 0.0, sf[r, at])
            return carry

        lax.fori_loop(0, 32, one, 0)
        res_next[...] = sf[...].astype(BF)


def next_residual(fb, fc, act, wd, res):
    nb = 1280
    return pl.pallas_call(
        residual_kernel,
        grid_spec=pltpu.PrefetchScalarGridSpec(
            num_scalar_prefetch=2,
            grid=(D // nb,),
            in_specs=[
                pl.BlockSpec((1, G, F), lambda n, *_: (2, 0, 0)),
                pl.BlockSpec((F, nb), lambda n, *_: (0, n)),
                pl.BlockSpec((G, nb), lambda n, *_: (0, n)),
            ],
            out_specs=pl.BlockSpec((G, D), lambda n, *_: (0, 0)),
            scratch_shapes=[pltpu.VMEM((G, D), F32)],
        ),
        out_shape=jax.ShapeDtypeStruct((G, D), BF),
        compiler_params=pltpu.CompilerParams(vmem_limit_bytes=VMEM_LIMIT),
        cost_estimate=pl.CostEstimate(
            flops=2 * G * F * D, bytes_accessed=2 * (2 * G * D + F * D), transcendentals=0
        ),
        name="next_residual",
    )(fb, fc, act, wd, res)


def unpack_kernel(idx, data, of, ob, pk, *accs):
    pk[...] = data[...].astype(F32)
    for acc in accs:
        acc[...] = jnp.zeros_like(acc)

    def one(i, carry):
        for j in range(KMAX):
            for q in range(4):
                t = (q // 2) * 16 + i
                back = q % 2
                at = pl.ds(pl.multiple_of(idx[t, back * KMAX + j] * 128, 128), 128)
                row = pl.multiple_of(t * MSG + back * 80 + j * 8, 8)
                accs[q][:, at] += pk[pl.ds(row, 8), :]
        return carry

    lax.fori_loop(0, 16, one, 0)
    of[...] = (accs[0][:, :D] + accs[2][:, :D]).astype(BF)
    ob[...] = (accs[1][:, :D] + accs[3][:, :D]).astype(BF)


def unpack(idx, data):
    whole = pl.BlockSpec(memory_space=pltpu.VMEM)
    return pl.pallas_call(
        unpack_kernel,
        in_specs=[pl.BlockSpec(memory_space=pltpu.SMEM), whole],
        out_specs=[whole, whole],
        out_shape=[jax.ShapeDtypeStruct((8, D), BF)] * 2,
        scratch_shapes=[
            pltpu.VMEM((32 * MSG, 128), F32),
        ]
        + [pltpu.VMEM((8, D + 128), F32)] * 4,
        compiler_params=pltpu.CompilerParams(vmem_limit_bytes=VMEM_LIMIT),
        cost_estimate=pl.CostEstimate(flops=10**6, bytes_accessed=2 * 10**6, transcendentals=0),
        name="unpack",
    )(idx, data)


def grads_kernel(core, act, *refs):
    far = refs[:16]
    og, ou, od, av, pv, acc, sem = refs[16:]
    copies = []
    for q in range(2):
        part = pl.ds(4 * q, 4)
        copies.append([pltpu.make_async_copy(act.at[part], av.at[part], sem.at[16 + q])])
        for i in (*range(4 * q, 4 * q + 4), *range(8 + 4 * q, 12 + 4 * q)):
            copies[-1].append(pltpu.make_async_copy(far[i], pv.at[i], sem.at[i]))
        for c in copies[-1]:
            c.start()

    def rows(first, s, n0, n1):
        blocks = []
        for i in range(4):
            for j in range(4):
                if s < 4:
                    blocks.append(pv[first + i, j, s, :, n0:n1])
                else:
                    blocks.append(pv[first + 4 + j, i, s - 4, :, n0:n1])
        return jnp.concatenate(blocks, axis=0)

    def run(q, tok, cot):
        for first, wanted in ((tok, ((0, og), (1, ou))), (cot, ((2, od),))):
            for n0, n1 in ((0, 256), (256, 512), (512, 640)):
                total = [None] * len(wanted)
                for s in range(4 * q, 4 * q + 4):
                    rhs = rows(first, s, n0, n1)
                    for w, (j, _) in enumerate(wanted):
                        term = nn(av[s, j], rhs)
                        total[w] = term if total[w] is None else total[w] + term
                for w, (j, out) in enumerate(wanted):
                    if q == 0:
                        acc[j, :, n0:n1] = total[w]
                    else:
                        out[:, n0:n1] = (acc[j, :, n0:n1] + total[w]).astype(BF)

    for q in range(2):
        for c in copies[q]:
            c.wait()

        @pl.when(core[0] == 0)
        def _():
            run(q, 0, 8)

        @pl.when(core[0] != 0)
        def _():
            run(q, 8, 0)


def grads(core, act, mine, other):
    whole = pl.BlockSpec(memory_space=pltpu.VMEM)
    return pl.pallas_call(
        grads_kernel,
        in_specs=[pl.BlockSpec(memory_space=pltpu.SMEM)] + [pl.BlockSpec(memory_space=pl.ANY)] * 17,
        out_specs=[whole] * 3,
        out_shape=[jax.ShapeDtypeStruct((F, 640), BF)] * 3,
        scratch_shapes=[
            pltpu.VMEM((8, 3, F, G), BF),
            pltpu.VMEM((16, 4, 4, 16, 640), BF),
            pltpu.VMEM((3, F, 640), F32),
            pltpu.SemaphoreType.DMA((18,)),
        ],
        compiler_params=pltpu.CompilerParams(vmem_limit_bytes=VMEM_LIMIT),
        cost_estimate=pl.CostEstimate(
            flops=6 * G * F * D, bytes_accessed=8 * 10**6, transcendentals=0
        ),
        name="grads",
    )(core, hbm(act), *[hbm(v) for v in (*mine, *other)])


def swap_core(v):
    return lax.ppermute(v, "core", [(0, 1), (1, 0)])


def shift(v, axis, size, by):
    return lax.ppermute(v, axis, [(i, (i + by) % size) for i in range(size)])


def shards(tok, wg, wu, wd, res, fb, fc, cot, bb, bc):
    core = lax.axis_index("core")
    first = core == 0
    which = core.astype(jnp.int32).reshape(1)
    fb, fc, bb, bc = fb[0, 0], fc[0, 0], bb[0, 0], bc[0, 0]

    rows = lax.all_gather(jnp.concatenate([tok, cot], axis=1), T, axis=0, tiled=True)

    other = swap_core(jnp.where(first, cot, tok))
    chip = jnp.concatenate([jnp.where(first, tok, other), jnp.where(first, other, cot)], axis=0)
    cols = lax.all_to_all(chip.reshape(16, 8, 640).transpose(1, 0, 2), "dp", 0, 0, tiled=True)
    halves = [cols[:4], cols[4:]]
    steps = [shift(halves[h], a, 4, s) for s in (2, 1, 3) for h, a in ((0, "x"), (1, "y"))]
    steps = lax.optimization_barrier(tuple(steps))
    four = [jnp.stack([halves[h], steps[2 + h], steps[h], steps[4 + h]]) for h in range(2)]
    four = lax.optimization_barrier(tuple(four))
    mine = [four[0], None, None, None, four[1], None, None, None]
    for s in (2, 1, 3):
        mine[s] = shift(four[0], "y", 4, s)
        mine[4 + s] = shift(four[1], "x", 4, s)
    rows, *mine = lax.optimization_barrier((rows, *mine))

    x, y = lax.axis_index("x"), lax.axis_index("y")
    a = jnp.arange(G)
    order = (((x - (a // 16) % 4) % 4) * 4 + (y - a // 64) % 4) * 16 + a % 16
    order = jnp.broadcast_to(order.astype(jnp.int32)[None], (8, G))
    slots = jnp.arange(KMAX)[None, :]
    lists = jnp.concatenate(
        [jnp.where(slots < fc[:, None], fb, 40), jnp.where(slots < bc[:, None], bb, 40)], axis=1
    )
    lists = jnp.broadcast_to(lists[:, None, :], (32, 16, 2 * KMAX))
    side = jnp.pad(lists, ((0, 0), (0, 0), (0, 128 - 2 * KMAX))).astype(F32)

    nat, act = acts(order, rows, wg, wu, wd)
    everyone = lax.all_gather(act[None], "dp", axis=0, tiled=True)
    payload = pack_selected(fb, bb, nat, side, wg, wu, wd, res[0, 0])
    payload, nat, *mine = lax.optimization_barrier((payload, nat, *mine))
    received = lax.all_to_all(payload, T, 0, 0, tiled=True)
    res_next = next_residual(fb, fc, nat, wd, res[0, 0])
    others = [swap_core(v) for v in mine]
    idx = received[:, 160, : 2 * KMAX].astype(jnp.int32)
    layer_output, input_gradient = unpack(idx, received.reshape(32 * MSG, 128))
    gate_gradient, up_gradient, down_gradient = grads(which, everyone, mine, others)
    return (
        layer_output,
        res_next[None, None],
        input_gradient,
        gate_gradient,
        up_gradient,
        down_gradient,
    )


def solution(mesh):
    fine = Mesh(mesh.devices.reshape(8, 4, 4, 2), ("dp", "x", "y", "core"))
    row = P(("dp",) + T, None)
    return jax.shard_map(
        shards,
        mesh=fine,
        in_specs=(
            row,
            P(T, None),
            P(T, None),
            P(T, None),
            P("dp", T, None, None),
            P("dp", T, None, None),
            P("dp", T, None),
            row,
            P("dp", T, None, None),
            P("dp", T, None),
        ),
        out_specs=(row, P("dp", T, None, None), row, P(T, "dp"), P(T, "dp"), P(T, "dp")),
        check_vma=False,
    )
```

```python
import jax
import jax.numpy as jnp
from jax import lax
from jax.experimental import pallas as pl
from jax.experimental.pallas import tpu as pltpu
from jax.sharding import Mesh, PartitionSpec as P

T = ("x", "y", "core")
XY = ("x", "y")
D = 5120
F = 216
G = 256
KMAX = 10
MSG = 176
VMEM_LIMIT = 56 << 20
BF = jnp.bfloat16
F32 = jnp.float32


def nt(a, b):
    return lax.dot_general(a, b, (((1,), (1,)), ((), ())), preferred_element_type=F32)


def tn(a, b):
    return lax.dot_general(a, b, (((0,), (0,)), ((), ())), preferred_element_type=F32)


def nn(a, b):
    return lax.dot_general(a, b, (((1,), (0,)), ((), ())), preferred_element_type=F32)


def acts_kernel(where, tok, cot, wg, wu, wd, nat, out, ga, ua, hb):
    k = pl.program_id(0)

    @pl.when(k == 0)
    def _():
        ga[...] = jnp.zeros_like(ga)
        ua[...] = jnp.zeros_like(ua)
        hb[...] = jnp.zeros_like(hb)

    t = tok[...]
    ga[...] += nt(t, wg[...])
    ua[...] += nt(t, wu[...])
    hb[...] += nt(cot[...], wd[...])

    @pl.when(k == pl.num_programs(0) - 1)
    def _():
        g, u, b = ga[...], ua[...], hb[...]
        s = jax.nn.sigmoid(g)
        silu = g * s
        at = lax.broadcasted_iota(jnp.int32, (G, G), 1)
        gx = (where[0] - ((at >> 4) & 3)) & 3
        gy = (where[1] - (at >> 6)) & 3
        order = ((gx * 4 + gy) << 4) + (at & 15)
        place = (lax.broadcasted_iota(jnp.int32, (G, G), 0) == order).astype(BF)
        values = (b * u * (s * (1.0 + g * (1.0 - s))), b * silu, silu * u)
        for j in range(3):
            v = values[j].astype(BF)
            nat[j] = v
            out[j] = tn(v, place).astype(BF)


def acts(where, rows, wg, wu, wd):
    kb = 2560
    steps = D // kb
    wspec = pl.BlockSpec((F, kb), lambda k: (0, k))
    return pl.pallas_call(
        acts_kernel,
        grid=(steps,),
        in_specs=[
            pl.BlockSpec(memory_space=pltpu.SMEM),
            pl.BlockSpec((G, kb), lambda k: (0, k)),
            pl.BlockSpec((G, kb), lambda k: (0, k + steps)),
            wspec,
            wspec,
            wspec,
        ],
        out_specs=[
            pl.BlockSpec((3, G, F), lambda k: (0, 0, 0)),
            pl.BlockSpec((3, F, G), lambda k: (0, 0, 0)),
        ],
        out_shape=[
            jax.ShapeDtypeStruct((3, G, F), BF),
            jax.ShapeDtypeStruct((3, F, G), BF),
        ],
        scratch_shapes=[pltpu.VMEM((G, F), F32)] * 3,
        compiler_params=pltpu.CompilerParams(vmem_limit_bytes=VMEM_LIMIT),
        cost_estimate=pl.CostEstimate(
            flops=6 * G * F * D, bytes_accessed=2 * (2 * G * D + 3 * F * D), transcendentals=G * F
        ),
        name="acts",
    )(where, rows, rows, wg, wu, wd)


def hbm(v):
    return pltpu.with_memory_space_constraint(v, pltpu.HBM)


CHUNK = 1280
CHUNKS = D // CHUNK


def pack_kernel(fb, bb, act, side, wg, wu, wd, res, payload, *scratch):
    vg, vu, vd, vr, sf, sb, pf, pb, po, sem = scratch
    loads = []
    for n, (far, near) in enumerate(((wg, vg), (wu, vu), (wd, vd), (res, vr))):
        loads.append([])
        for k in range(CHUNKS):
            cols = pl.ds(k * CHUNK, CHUNK)
            at = sem.at[n * CHUNKS + k]
            loads[-1].append(pltpu.make_async_copy(far.at[:, cols], near.at[:, cols], at))
    for pair in (loads[:2], loads[2:]):
        for k in range(CHUNKS):
            pair[0][k].start()
            pair[1][k].start()

    def pack(blocks, source, packed):
        def one(t, carry):
            r = pl.ds(pl.multiple_of(t * 8, 8), 8)
            for j in range(KMAX):
                at = pl.ds(pl.multiple_of(blocks[t, j] * 128, 128), 128)
                packed[t, j * 8 : j * 8 + 8, :] = source[r, at]
            return carry

        lax.fori_loop(0, 32, one, 0)

    def send(i, lo, hi):
        part = pl.ds(lo, hi - lo)
        return pltpu.make_async_copy(
            po.at[:, part, :], payload.at[:, part, :], sem.at[4 * CHUNKS + i]
        )

    for k in range(CHUNKS):
        cols = pl.ds(k * CHUNK, CHUNK)
        loads[0][k].wait()
        loads[1][k].wait()
        sb[:, cols] = nn(act[0], vg[:, cols]) + nn(act[1], vu[:, cols])
    pack(bb, sb, pb)
    po[:, 80:160, :] = pb[...].astype(BF)
    po[:, 160:MSG, :] = side[...].astype(BF)
    back = send(0, 80, MSG)
    back.start()
    for k in range(CHUNKS):
        cols = pl.ds(k * CHUNK, CHUNK)
        loads[2][k].wait()
        loads[3][k].wait()
        sf[:, cols] = nn(act[2], vd[:, cols]) + vr[:, cols].astype(F32)
    pack(fb, sf, pf)
    po[:, 0:80, :] = pf[...].astype(BF)
    ahead = send(1, 0, 80)
    ahead.start()
    back.wait()
    ahead.wait()


def pack_selected(fb, bb, act, side, wg, wu, wd, res):
    whole = pl.BlockSpec(memory_space=pltpu.VMEM)
    smem = pl.BlockSpec(memory_space=pltpu.SMEM)
    anywhere = pl.BlockSpec(memory_space=pl.ANY)
    return pl.pallas_call(
        pack_kernel,
        in_specs=[smem] * 2 + [whole] * 2 + [anywhere] * 4,
        out_specs=anywhere,
        out_shape=pltpu.HBM((32, MSG, 128), BF),
        scratch_shapes=[pltpu.VMEM((F, D), BF)] * 3
        + [
            pltpu.VMEM((G, D), BF),
            pltpu.VMEM((G, D), F32),
            pltpu.VMEM((G, D), F32),
            pltpu.VMEM((32, 80, 128), F32),
            pltpu.VMEM((32, 80, 128), F32),
            pltpu.VMEM((32, MSG, 128), BF),
            pltpu.SemaphoreType.DMA((4 * CHUNKS + 2,)),
        ],
        compiler_params=pltpu.CompilerParams(vmem_limit_bytes=VMEM_LIMIT),
        cost_estimate=pl.CostEstimate(
            flops=6 * G * F * D, bytes_accessed=2 * (G * D + 3 * F * D), transcendentals=0
        ),
        name="pack_selected",
    )(fb, bb, act, side, hbm(wg), hbm(wu), hbm(wd), hbm(res))


def residual_kernel(fb, fc, act, wd, res, res_next, sf):
    n = pl.program_id(0)
    nb = wd.shape[1]
    cols = pl.ds(pl.multiple_of(n * nb, nb), nb)
    sf[:, cols] = nn(act[0], wd[...]) + res[...].astype(F32)

    @pl.when(n == pl.num_programs(0) - 1)
    def _():
        def one(t, carry):
            r = pl.ds(pl.multiple_of(t * 8, 8), 8)
            count = fc[t]
            for j in range(KMAX):
                at = pl.ds(pl.multiple_of(fb[t, j] * 128, 128), 128)
                sf[r, at] = jnp.where(j < count, 0.0, sf[r, at])
            return carry

        lax.fori_loop(0, 32, one, 0)
        res_next[...] = sf[...].astype(BF)


def next_residual(fb, fc, act, wd, res):
    nb = 1280
    return pl.pallas_call(
        residual_kernel,
        grid_spec=pltpu.PrefetchScalarGridSpec(
            num_scalar_prefetch=2,
            grid=(D // nb,),
            in_specs=[
                pl.BlockSpec((1, G, F), lambda n, *_: (2, 0, 0)),
                pl.BlockSpec((F, nb), lambda n, *_: (0, n)),
                pl.BlockSpec((G, nb), lambda n, *_: (0, n)),
            ],
            out_specs=pl.BlockSpec((G, D), lambda n, *_: (0, 0)),
            scratch_shapes=[pltpu.VMEM((G, D), F32)],
        ),
        out_shape=jax.ShapeDtypeStruct((G, D), BF),
        compiler_params=pltpu.CompilerParams(vmem_limit_bytes=VMEM_LIMIT),
        cost_estimate=pl.CostEstimate(
            flops=2 * G * F * D, bytes_accessed=2 * (2 * G * D + F * D), transcendentals=0
        ),
        name="next_residual",
    )(fb, fc, act, wd, res)


def unpack_kernel(idx, data, of, ob, pk, *accs):
    pk[...] = data[...].astype(F32)
    for acc in accs:
        acc[...] = jnp.zeros_like(acc)

    def one(i, carry):
        for j in range(KMAX):
            for q in range(4):
                t = (q // 2) * 16 + i
                back = q % 2
                at = pl.ds(pl.multiple_of(idx[t, back * KMAX + j] * 128, 128), 128)
                row = pl.multiple_of(t * MSG + back * 80 + j * 8, 8)
                accs[q][:, at] += pk[pl.ds(row, 8), :]
        return carry

    lax.fori_loop(0, 16, one, 0)
    of[...] = (accs[0][:, :D] + accs[2][:, :D]).astype(BF)
    ob[...] = (accs[1][:, :D] + accs[3][:, :D]).astype(BF)


def unpack(idx, data):
    whole = pl.BlockSpec(memory_space=pltpu.VMEM)
    return pl.pallas_call(
        unpack_kernel,
        in_specs=[pl.BlockSpec(memory_space=pltpu.SMEM), whole],
        out_specs=[whole, whole],
        out_shape=[jax.ShapeDtypeStruct((8, D), BF)] * 2,
        scratch_shapes=[
            pltpu.VMEM((32 * MSG, 128), F32),
        ]
        + [pltpu.VMEM((8, D + 128), F32)] * 4,
        compiler_params=pltpu.CompilerParams(vmem_limit_bytes=VMEM_LIMIT),
        cost_estimate=pl.CostEstimate(flops=10**6, bytes_accessed=2 * 10**6, transcendentals=0),
        name="unpack",
    )(idx, data)


def grads_kernel(core, act, *refs):
    far = refs[:16]
    og, ou, od, av, pv, acc, sem = refs[16:]
    copies = []
    for q in range(2):
        part = pl.ds(4 * q, 4)
        copies.append([pltpu.make_async_copy(act.at[part], av.at[part], sem.at[16 + q])])
        for i in (*range(4 * q, 4 * q + 4), *range(8 + 4 * q, 12 + 4 * q)):
            copies[-1].append(pltpu.make_async_copy(far[i], pv.at[i], sem.at[i]))
        for c in copies[-1]:
            c.start()

    def rows(first, s, n0, n1):
        blocks = []
        for i in range(4):
            for j in range(4):
                if s < 4:
                    blocks.append(pv[first + i, j, s, :, n0:n1])
                else:
                    blocks.append(pv[first + 4 + j, i, s - 4, :, n0:n1])
        return jnp.concatenate(blocks, axis=0)

    def run(q, tok, cot):
        for first, wanted in ((tok, ((0, og), (1, ou))), (cot, ((2, od),))):
            for n0, n1 in ((0, 256), (256, 512), (512, 640)):
                total = [None] * len(wanted)
                for s in range(4 * q, 4 * q + 4):
                    rhs = rows(first, s, n0, n1)
                    for w, (j, _) in enumerate(wanted):
                        term = nn(av[s, j], rhs)
                        total[w] = term if total[w] is None else total[w] + term
                for w, (j, out) in enumerate(wanted):
                    if q == 0:
                        acc[j, :, n0:n1] = total[w]
                    else:
                        out[:, n0:n1] = (acc[j, :, n0:n1] + total[w]).astype(BF)

    for q in range(2):
        for c in copies[q]:
            c.wait()

        @pl.when(core[0] == 0)
        def _():
            run(q, 0, 8)

        @pl.when(core[0] != 0)
        def _():
            run(q, 8, 0)


def grads(core, act, mine, other):
    whole = pl.BlockSpec(memory_space=pltpu.VMEM)
    return pl.pallas_call(
        grads_kernel,
        in_specs=[pl.BlockSpec(memory_space=pltpu.SMEM)] + [pl.BlockSpec(memory_space=pl.ANY)] * 17,
        out_specs=[whole] * 3,
        out_shape=[jax.ShapeDtypeStruct((F, 640), BF)] * 3,
        scratch_shapes=[
            pltpu.VMEM((8, 3, F, G), BF),
            pltpu.VMEM((16, 4, 4, 16, 640), BF),
            pltpu.VMEM((3, F, 640), F32),
            pltpu.SemaphoreType.DMA((18,)),
        ],
        compiler_params=pltpu.CompilerParams(vmem_limit_bytes=VMEM_LIMIT),
        cost_estimate=pl.CostEstimate(
            flops=6 * G * F * D, bytes_accessed=8 * 10**6, transcendentals=0
        ),
        name="grads",
    )(core, hbm(act), *[hbm(v) for v in (*mine, *other)])


def swap_core(v):
    return lax.ppermute(v, "core", [(0, 1), (1, 0)])


def shift(v, axis, size, by):
    return lax.ppermute(v, axis, [(i, (i + by) % size) for i in range(size)])


def shards(tok, wg, wu, wd, res, fb, fc, cot, bb, bc):
    core = lax.axis_index("core")
    which = core.astype(jnp.int32).reshape(1)
    fb, fc, bb, bc = fb[0, 0], fc[0, 0], bb[0, 0], bc[0, 0]

    rows = lax.all_gather(jnp.concatenate([tok, cot], axis=1), T, axis=0, tiled=True)

    blocks = [v.reshape(8, 8, 640).transpose(1, 0, 2) for v in (tok, cot)]
    blocks = jnp.stack(blocks, axis=1).reshape(16, 8, 640)
    cols = lax.all_to_all(blocks, ("dp", "core"), 0, 0, tiled=True).reshape(8, 16, 640)
    halves = [cols[:4], cols[4:]]
    steps = [shift(halves[h], a, 4, s) for s in (1, 3) for h, a in ((0, "x"), (1, "y"))]
    steps = [shift(steps[0], "x", 4, 1), shift(steps[1], "y", 4, 1), *steps]
    steps = lax.optimization_barrier(tuple(steps))
    four = [jnp.stack([halves[h], steps[2 + h], steps[h], steps[4 + h]]) for h in range(2)]
    slots = jnp.arange(KMAX)[None, :]
    lists = jnp.concatenate(
        [jnp.where(slots < fc[:, None], fb, 40), jnp.where(slots < bc[:, None], bb, 40)], axis=1
    )
    lists = jnp.broadcast_to(lists[:, None, :], (32, 16, 2 * KMAX))
    side = jnp.pad(lists, ((0, 0), (0, 0), (0, 128 - 2 * KMAX))).astype(F32)
    *four, side = lax.optimization_barrier((*four, side))
    mine = [four[0], None, None, None, four[1], None, None, None]
    for s in (1, 3):
        mine[s] = shift(four[0], "y", 4, s)
        mine[4 + s] = shift(four[1], "x", 4, s)
    mine[2], mine[6] = shift(mine[3], "y", 4, -1), shift(mine[7], "x", 4, -1)
    rows, *mine = lax.optimization_barrier((rows, *mine))

    where = jnp.stack([lax.axis_index("x"), lax.axis_index("y")]).astype(jnp.int32)
    nat, act = acts(where, rows, wg, wu, wd)
    everyone = lax.all_gather(act[None], "dp", axis=0, tiled=True)
    payload = pack_selected(fb, bb, nat, side, wg, wu, wd, res[0, 0])
    payload, nat, *mine = lax.optimization_barrier((payload, nat, *mine))
    received = lax.all_to_all(payload, T, 0, 0, tiled=True)
    res_next = next_residual(fb, fc, nat, wd, res[0, 0])
    others = [swap_core(v) for v in mine]
    idx = received[:, 160, : 2 * KMAX].astype(jnp.int32)
    layer_output, input_gradient = unpack(idx, received.reshape(32 * MSG, 128))
    gate_gradient, up_gradient, down_gradient = grads(which, everyone, mine, others)
    return (
        layer_output,
        res_next[None, None],
        input_gradient,
        gate_gradient,
        up_gradient,
        down_gradient,
    )


def solution(mesh):
    fine = Mesh(mesh.devices.reshape(8, 4, 4, 2), ("dp", "x", "y", "core"))
    row = P(("dp",) + T, None)
    return jax.shard_map(
        shards,
        mesh=fine,
        in_specs=(
            row,
            P(T, None),
            P(T, None),
            P(T, None),
            P("dp", T, None, None),
            P("dp", T, None, None),
            P("dp", T, None),
            row,
            P("dp", T, None, None),
            P("dp", T, None),
        ),
        out_specs=(row, P("dp", T, None, None), row, P(T, "dp"), P(T, "dp"), P(T, "dp")),
        check_vma=False,
    )
```

```python
import jax
import jax.numpy as jnp
from jax import lax
from jax.experimental import pallas as pl
from jax.experimental.pallas import tpu as pltpu
from jax.sharding import Mesh, PartitionSpec as P

T = ("x", "y", "core")
XY = ("x", "y")
D = 5120
F = 216
G = 256
KMAX = 10
MSG = 176
VMEM_LIMIT = 56 << 20
BF = jnp.bfloat16
F32 = jnp.float32


def nt(a, b):
    return lax.dot_general(a, b, (((1,), (1,)), ((), ())), preferred_element_type=F32)


def tn(a, b):
    return lax.dot_general(a, b, (((0,), (0,)), ((), ())), preferred_element_type=F32)


def nn(a, b):
    return lax.dot_general(a, b, (((1,), (0,)), ((), ())), preferred_element_type=F32)


def acts_kernel(where, tok, cot, wg, wu, wd, nat, out, ga, ua, hb):
    k = pl.program_id(0)

    @pl.when(k == 0)
    def _():
        ga[...] = jnp.zeros_like(ga)
        ua[...] = jnp.zeros_like(ua)
        hb[...] = jnp.zeros_like(hb)

    t = tok[...]
    ga[...] += nt(t, wg[...])
    ua[...] += nt(t, wu[...])
    hb[...] += nt(cot[...], wd[...])

    @pl.when(k == pl.num_programs(0) - 1)
    def _():
        g, u, b = ga[...], ua[...], hb[...]
        s = jax.nn.sigmoid(g)
        silu = g * s
        at = lax.broadcasted_iota(jnp.int32, (G, G), 1)
        gx = (where[0] - ((at >> 4) & 3)) & 3
        gy = (where[1] - (at >> 6)) & 3
        order = ((gx * 4 + gy) << 4) + (at & 15)
        place = (lax.broadcasted_iota(jnp.int32, (G, G), 0) == order).astype(BF)
        values = (b * u * (s * (1.0 + g * (1.0 - s))), b * silu, silu * u)
        for j in range(3):
            v = values[j].astype(BF)
            nat[j] = v
            out[j] = tn(v, place).astype(BF)


def acts(where, rows, wg, wu, wd):
    kb = 2560
    steps = D // kb
    wspec = pl.BlockSpec((F, kb), lambda k: (0, k))
    return pl.pallas_call(
        acts_kernel,
        grid=(steps,),
        in_specs=[
            pl.BlockSpec(memory_space=pltpu.SMEM),
            pl.BlockSpec((G, kb), lambda k: (0, k)),
            pl.BlockSpec((G, kb), lambda k: (0, k + steps)),
            wspec,
            wspec,
            wspec,
        ],
        out_specs=[
            pl.BlockSpec((3, G, F), lambda k: (0, 0, 0)),
            pl.BlockSpec((3, F, G), lambda k: (0, 0, 0)),
        ],
        out_shape=[
            jax.ShapeDtypeStruct((3, G, F), BF),
            jax.ShapeDtypeStruct((3, F, G), BF),
        ],
        scratch_shapes=[pltpu.VMEM((G, F), F32)] * 3,
        compiler_params=pltpu.CompilerParams(vmem_limit_bytes=VMEM_LIMIT),
        cost_estimate=pl.CostEstimate(
            flops=6 * G * F * D, bytes_accessed=2 * (2 * G * D + 3 * F * D), transcendentals=G * F
        ),
        name="acts",
    )(where, rows, rows, wg, wu, wd)


def hbm(v):
    return pltpu.with_memory_space_constraint(v, pltpu.HBM)


CHUNK = 1280
CHUNKS = D // CHUNK


def pack_kernel(fb, bb, act, side, wg, wu, wd, res, payload, *scratch):
    vg, vu, vd, vr, sf, sb, pf, pb, po, sem = scratch
    loads = []
    for n, (far, near) in enumerate(((wg, vg), (wu, vu), (wd, vd), (res, vr))):
        loads.append([])
        for k in range(CHUNKS):
            cols = pl.ds(k * CHUNK, CHUNK)
            at = sem.at[n * CHUNKS + k]
            loads[-1].append(pltpu.make_async_copy(far.at[:, cols], near.at[:, cols], at))
    for pair in (loads[:2], loads[2:]):
        for k in range(CHUNKS):
            pair[0][k].start()
            pair[1][k].start()

    def pack(blocks, source, packed):
        def one(t, carry):
            r = pl.ds(pl.multiple_of(t * 8, 8), 8)
            for j in range(KMAX):
                at = pl.ds(pl.multiple_of(blocks[t, j] * 128, 128), 128)
                packed[t, j * 8 : j * 8 + 8, :] = source[r, at]
            return carry

        lax.fori_loop(0, 32, one, 0)

    def send(i, lo, hi):
        part = pl.ds(lo, hi - lo)
        return pltpu.make_async_copy(
            po.at[:, part, :], payload.at[:, part, :], sem.at[4 * CHUNKS + i]
        )

    for k in range(CHUNKS):
        cols = pl.ds(k * CHUNK, CHUNK)
        loads[0][k].wait()
        loads[1][k].wait()
        sb[:, cols] = nn(act[0], vg[:, cols]) + nn(act[1], vu[:, cols])
    pack(bb, sb, pb)
    po[:, 80:160, :] = pb[...].astype(BF)
    po[:, 160:MSG, :] = side[...].astype(BF)
    back = send(0, 80, MSG)
    back.start()
    for k in range(CHUNKS):
        cols = pl.ds(k * CHUNK, CHUNK)
        loads[2][k].wait()
        loads[3][k].wait()
        sf[:, cols] = nn(act[2], vd[:, cols]) + vr[:, cols].astype(F32)
    pack(fb, sf, pf)
    po[:, 0:80, :] = pf[...].astype(BF)
    ahead = send(1, 0, 80)
    ahead.start()
    back.wait()
    ahead.wait()


def pack_selected(fb, bb, act, side, wg, wu, wd, res):
    whole = pl.BlockSpec(memory_space=pltpu.VMEM)
    smem = pl.BlockSpec(memory_space=pltpu.SMEM)
    anywhere = pl.BlockSpec(memory_space=pl.ANY)
    return pl.pallas_call(
        pack_kernel,
        in_specs=[smem] * 2 + [whole] * 2 + [anywhere] * 4,
        out_specs=anywhere,
        out_shape=pltpu.HBM((32, MSG, 128), BF),
        scratch_shapes=[pltpu.VMEM((F, D), BF)] * 3
        + [
            pltpu.VMEM((G, D), BF),
            pltpu.VMEM((G, D), F32),
            pltpu.VMEM((G, D), F32),
            pltpu.VMEM((32, 80, 128), F32),
            pltpu.VMEM((32, 80, 128), F32),
            pltpu.VMEM((32, MSG, 128), BF),
            pltpu.SemaphoreType.DMA((4 * CHUNKS + 2,)),
        ],
        compiler_params=pltpu.CompilerParams(vmem_limit_bytes=VMEM_LIMIT),
        cost_estimate=pl.CostEstimate(
            flops=6 * G * F * D, bytes_accessed=2 * (G * D + 3 * F * D), transcendentals=0
        ),
        name="pack_selected",
    )(fb, bb, act, side, hbm(wg), hbm(wu), hbm(wd), hbm(res))


def residual_kernel(fb, fc, act, wd, res, res_next, sf):
    n = pl.program_id(0)
    nb = wd.shape[1]
    cols = pl.ds(pl.multiple_of(n * nb, nb), nb)
    sf[:, cols] = nn(act[0], wd[...]) + res[...].astype(F32)

    @pl.when(n == pl.num_programs(0) - 1)
    def _():
        def one(t, carry):
            r = pl.ds(pl.multiple_of(t * 8, 8), 8)
            count = fc[t]
            for j in range(KMAX):
                at = pl.ds(pl.multiple_of(fb[t, j] * 128, 128), 128)
                sf[r, at] = jnp.where(j < count, 0.0, sf[r, at])
            return carry

        lax.fori_loop(0, 32, one, 0)
        res_next[...] = sf[...].astype(BF)


def next_residual(fb, fc, act, wd, res):
    nb = 1280
    return pl.pallas_call(
        residual_kernel,
        grid_spec=pltpu.PrefetchScalarGridSpec(
            num_scalar_prefetch=2,
            grid=(D // nb,),
            in_specs=[
                pl.BlockSpec((1, G, F), lambda n, *_: (2, 0, 0)),
                pl.BlockSpec((F, nb), lambda n, *_: (0, n)),
                pl.BlockSpec((G, nb), lambda n, *_: (0, n)),
            ],
            out_specs=pl.BlockSpec((G, D), lambda n, *_: (0, 0)),
            scratch_shapes=[pltpu.VMEM((G, D), F32)],
        ),
        out_shape=jax.ShapeDtypeStruct((G, D), BF),
        compiler_params=pltpu.CompilerParams(vmem_limit_bytes=VMEM_LIMIT),
        cost_estimate=pl.CostEstimate(
            flops=2 * G * F * D, bytes_accessed=2 * (2 * G * D + F * D), transcendentals=0
        ),
        name="next_residual",
    )(fb, fc, act, wd, res)


def unpack_kernel(idx, data, of, ob, pk, *accs):
    pk[...] = data[...].astype(F32)
    for acc in accs:
        acc[...] = jnp.zeros_like(acc)

    def one(i, carry):
        for j in range(KMAX):
            for q in range(4):
                t = (q // 2) * 16 + i
                back = q % 2
                at = pl.ds(pl.multiple_of(idx[t, back * KMAX + j] * 128, 128), 128)
                row = pl.multiple_of(t * MSG + back * 80 + j * 8, 8)
                accs[q][:, at] += pk[pl.ds(row, 8), :]
        return carry

    lax.fori_loop(0, 16, one, 0)
    of[...] = (accs[0][:, :D] + accs[2][:, :D]).astype(BF)
    ob[...] = (accs[1][:, :D] + accs[3][:, :D]).astype(BF)


def unpack(idx, data):
    whole = pl.BlockSpec(memory_space=pltpu.VMEM)
    return pl.pallas_call(
        unpack_kernel,
        in_specs=[pl.BlockSpec(memory_space=pltpu.SMEM), whole],
        out_specs=[whole, whole],
        out_shape=[jax.ShapeDtypeStruct((8, D), BF)] * 2,
        scratch_shapes=[
            pltpu.VMEM((32 * MSG, 128), F32),
        ]
        + [pltpu.VMEM((8, D + 128), F32)] * 4,
        compiler_params=pltpu.CompilerParams(vmem_limit_bytes=12 << 20),
        cost_estimate=pl.CostEstimate(flops=10**6, bytes_accessed=2 * 10**6, transcendentals=0),
        name="unpack",
    )(idx, data)


def grads_kernel(core, act, *refs):
    far = refs[:16]
    og, ou, od, av, pv, acc, sem = refs[16:]
    copies = []
    for q in range(2):
        part = pl.ds(4 * q, 4)
        copies.append([pltpu.make_async_copy(act.at[part], av.at[part], sem.at[16 + q])])
        for i in (*range(4 * q, 4 * q + 4), *range(8 + 4 * q, 12 + 4 * q)):
            copies[-1].append(pltpu.make_async_copy(far[i], pv.at[i], sem.at[i]))
        for c in copies[-1]:
            c.start()

    def rows(first, s, n0, n1):
        blocks = []
        for i in range(4):
            for j in range(4):
                if s < 4:
                    blocks.append(pv[first + i, j, s, :, n0:n1])
                else:
                    blocks.append(pv[first + 4 + j, i, s - 4, :, n0:n1])
        return jnp.concatenate(blocks, axis=0)

    def run(q, tok, cot):
        for first, wanted in ((tok, ((0, og), (1, ou))), (cot, ((2, od),))):
            for n0, n1 in ((0, 256), (256, 512), (512, 640)):
                total = [None] * len(wanted)
                for s in range(4 * q, 4 * q + 4):
                    rhs = rows(first, s, n0, n1)
                    for w, (j, _) in enumerate(wanted):
                        term = nn(av[s, j], rhs)
                        total[w] = term if total[w] is None else total[w] + term
                for w, (j, out) in enumerate(wanted):
                    if q == 0:
                        acc[j, :, n0:n1] = total[w]
                    else:
                        out[:, n0:n1] = (acc[j, :, n0:n1] + total[w]).astype(BF)

    for q in range(2):
        for c in copies[q]:
            c.wait()

        @pl.when(core[0] == 0)
        def _():
            run(q, 0, 8)

        @pl.when(core[0] != 0)
        def _():
            run(q, 8, 0)


def grads(core, act, mine, other):
    whole = pl.BlockSpec(memory_space=pltpu.VMEM)
    return pl.pallas_call(
        grads_kernel,
        in_specs=[pl.BlockSpec(memory_space=pltpu.SMEM)] + [pl.BlockSpec(memory_space=pl.ANY)] * 17,
        out_specs=[whole] * 3,
        out_shape=[jax.ShapeDtypeStruct((F, 640), BF)] * 3,
        scratch_shapes=[
            pltpu.VMEM((8, 3, F, G), BF),
            pltpu.VMEM((16, 4, 4, 16, 640), BF),
            pltpu.VMEM((3, F, 640), F32),
            pltpu.SemaphoreType.DMA((18,)),
        ],
        compiler_params=pltpu.CompilerParams(vmem_limit_bytes=VMEM_LIMIT),
        cost_estimate=pl.CostEstimate(
            flops=6 * G * F * D, bytes_accessed=8 * 10**6, transcendentals=0
        ),
        name="grads",
    )(core, hbm(act), *[hbm(v) for v in (*mine, *other)])


def swap_core(v):
    return lax.ppermute(v, "core", [(0, 1), (1, 0)])


def shift(v, axis, size, by):
    return lax.ppermute(v, axis, [(i, (i + by) % size) for i in range(size)])


def shards(tok, wg, wu, wd, res, fb, fc, cot, bb, bc):
    core = lax.axis_index("core")
    which = core.astype(jnp.int32).reshape(1)
    fb, fc, bb, bc = fb[0, 0], fc[0, 0], bb[0, 0], bc[0, 0]

    rows = lax.all_gather(jnp.concatenate([tok, cot], axis=1), T, axis=0, tiled=True)

    blocks = [v.reshape(8, 8, 640).transpose(1, 0, 2) for v in (tok, cot)]
    blocks = jnp.stack(blocks, axis=1).reshape(16, 8, 640)
    cols = lax.all_to_all(blocks, ("dp", "core"), 0, 0, tiled=True).reshape(8, 16, 640)
    halves = [cols[:4], cols[4:]]
    steps = [shift(halves[h], a, 4, s) for s in (1, 3) for h, a in ((0, "x"), (1, "y"))]
    steps = [shift(steps[0], "x", 4, 1), shift(steps[1], "y", 4, 1), *steps]
    steps = lax.optimization_barrier(tuple(steps))
    four = [jnp.stack([halves[h], steps[2 + h], steps[h], steps[4 + h]]) for h in range(2)]
    slots = jnp.arange(KMAX)[None, :]
    lists = jnp.concatenate(
        [jnp.where(slots < fc[:, None], fb, 40), jnp.where(slots < bc[:, None], bb, 40)], axis=1
    )
    lists = jnp.broadcast_to(lists[:, None, :], (32, 16, 2 * KMAX))
    side = jnp.pad(lists, ((0, 0), (0, 0), (0, 128 - 2 * KMAX))).astype(F32)
    *four, side = lax.optimization_barrier((*four, side))
    mine = [four[0], None, None, None, four[1], None, None, None]
    for s in (1, 3):
        mine[s] = shift(four[0], "y", 4, s)
        mine[4 + s] = shift(four[1], "x", 4, s)
    mine[2], mine[6] = shift(mine[3], "y", 4, -1), shift(mine[7], "x", 4, -1)
    rows, *mine = lax.optimization_barrier((rows, *mine))

    where = jnp.stack([lax.axis_index("x"), lax.axis_index("y")]).astype(jnp.int32)
    nat, act = acts(where, rows, wg, wu, wd)
    everyone = lax.all_gather(act[None], "dp", axis=0, tiled=True)
    payload = pack_selected(fb, bb, nat, side, wg, wu, wd, res[0, 0])
    payload, nat, *mine = lax.optimization_barrier((payload, nat, *mine))
    received = lax.all_to_all(payload, T, 0, 0, tiled=True)
    others = [swap_core(v) for v in mine]
    nat, *others = lax.optimization_barrier((nat, *others))
    res_next = next_residual(fb, fc, nat, wd, res[0, 0])
    idx = received[:, 160, : 2 * KMAX].astype(jnp.int32)
    layer_output, input_gradient = unpack(idx, received.reshape(32 * MSG, 128))
    gate_gradient, up_gradient, down_gradient = grads(which, everyone, mine, others)
    return (
        layer_output,
        res_next[None, None],
        input_gradient,
        gate_gradient,
        up_gradient,
        down_gradient,
    )


def solution(mesh):
    fine = Mesh(mesh.devices.reshape(8, 4, 4, 2), ("dp", "x", "y", "core"))
    row = P(("dp",) + T, None)
    return jax.shard_map(
        shards,
        mesh=fine,
        in_specs=(
            row,
            P(T, None),
            P(T, None),
            P(T, None),
            P("dp", T, None, None),
            P("dp", T, None, None),
            P("dp", T, None),
            row,
            P("dp", T, None, None),
            P("dp", T, None),
        ),
        out_specs=(row, P("dp", T, None, None), row, P(T, "dp"), P(T, "dp"), P(T, "dp")),
        check_vma=False,
    )
```

```python
import jax
import jax.numpy as jnp
from jax import lax
from jax.experimental import pallas as pl
from jax.experimental.pallas import tpu as pltpu
from jax.sharding import Mesh, PartitionSpec as P

T = ("x", "y", "core")
XY = ("x", "y")
D = 5120
F = 216
G = 256
KMAX = 10
MSG = 176
VMEM_LIMIT = 56 << 20
BF = jnp.bfloat16
F32 = jnp.float32


def nt(a, b):
    return lax.dot_general(a, b, (((1,), (1,)), ((), ())), preferred_element_type=F32)


def tn(a, b):
    return lax.dot_general(a, b, (((0,), (0,)), ((), ())), preferred_element_type=F32)


def nn(a, b):
    return lax.dot_general(a, b, (((1,), (0,)), ((), ())), preferred_element_type=F32)


def acts_kernel(where, tok, cot, wg, wu, wd, nat, out, ga, ua, hb):
    k = pl.program_id(0)

    @pl.when(k == 0)
    def _():
        ga[...] = jnp.zeros_like(ga)
        ua[...] = jnp.zeros_like(ua)
        hb[...] = jnp.zeros_like(hb)

    t = tok[...]
    ga[...] += nt(t, wg[...])
    ua[...] += nt(t, wu[...])
    hb[...] += nt(cot[...], wd[...])

    @pl.when(k == pl.num_programs(0) - 1)
    def _():
        g, u, b = ga[...], ua[...], hb[...]
        s = jax.nn.sigmoid(g)
        silu = g * s
        at = lax.broadcasted_iota(jnp.int32, (G, G), 1)
        gx = (where[0] - ((at >> 4) & 3)) & 3
        gy = (where[1] - (at >> 6)) & 3
        order = ((gx * 4 + gy) << 4) + (at & 15)
        place = (lax.broadcasted_iota(jnp.int32, (G, G), 0) == order).astype(BF)
        values = (b * u * (s * (1.0 + g * (1.0 - s))), b * silu, silu * u)
        for j in range(3):
            v = values[j].astype(BF)
            nat[j] = v
            out[j] = tn(v, place).astype(BF)


def acts(where, rows, wg, wu, wd):
    kb = 2560
    steps = D // kb
    wspec = pl.BlockSpec((F, kb), lambda k: (0, k))
    return pl.pallas_call(
        acts_kernel,
        grid=(steps,),
        in_specs=[
            pl.BlockSpec(memory_space=pltpu.SMEM),
            pl.BlockSpec((G, kb), lambda k: (0, k)),
            pl.BlockSpec((G, kb), lambda k: (0, k + steps)),
            wspec,
            wspec,
            wspec,
        ],
        out_specs=[
            pl.BlockSpec((3, G, F), lambda k: (0, 0, 0)),
            pl.BlockSpec((3, F, G), lambda k: (0, 0, 0)),
        ],
        out_shape=[
            jax.ShapeDtypeStruct((3, G, F), BF),
            jax.ShapeDtypeStruct((3, F, G), BF),
        ],
        scratch_shapes=[pltpu.VMEM((G, F), F32)] * 3,
        compiler_params=pltpu.CompilerParams(vmem_limit_bytes=24 << 20),
        cost_estimate=pl.CostEstimate(
            flops=6 * G * F * D, bytes_accessed=2 * (2 * G * D + 3 * F * D), transcendentals=G * F
        ),
        name="acts",
    )(where, hbm(rows), hbm(rows), hbm(wg), hbm(wu), hbm(wd))


def hbm(v):
    return pltpu.with_memory_space_constraint(v, pltpu.HBM)


CHUNK = 1280
CHUNKS = D // CHUNK


def pack_kernel(fb, bb, act, side, wg, wu, wd, res, payload, *scratch):
    vg, vu, vd, vr, sf, sb, pf, pb, po, sem = scratch
    loads = []
    for n, (far, near) in enumerate(((wg, vg), (wu, vu), (wd, vd), (res, vr))):
        loads.append([])
        for k in range(CHUNKS):
            cols = pl.ds(k * CHUNK, CHUNK)
            at = sem.at[n * CHUNKS + k]
            loads[-1].append(pltpu.make_async_copy(far.at[:, cols], near.at[:, cols], at))
    for pair in (loads[:2], loads[2:]):
        for k in range(CHUNKS):
            pair[0][k].start()
            pair[1][k].start()

    def pack(blocks, source, packed):
        def one(t, carry):
            r = pl.ds(pl.multiple_of(t * 8, 8), 8)
            for j in range(KMAX):
                at = pl.ds(pl.multiple_of(blocks[t, j] * 128, 128), 128)
                packed[t, j * 8 : j * 8 + 8, :] = source[r, at]
            return carry

        lax.fori_loop(0, 32, one, 0)

    def send(i, lo, hi):
        part = pl.ds(lo, hi - lo)
        return pltpu.make_async_copy(
            po.at[:, part, :], payload.at[:, part, :], sem.at[4 * CHUNKS + i]
        )

    for k in range(CHUNKS):
        cols = pl.ds(k * CHUNK, CHUNK)
        loads[0][k].wait()
        loads[1][k].wait()
        sb[:, cols] = nn(act[0], vg[:, cols]) + nn(act[1], vu[:, cols])
    pack(bb, sb, pb)
    po[:, 80:160, :] = pb[...].astype(BF)
    po[:, 160:MSG, :] = side[...].astype(BF)
    back = send(0, 80, MSG)
    back.start()
    for k in range(CHUNKS):
        cols = pl.ds(k * CHUNK, CHUNK)
        loads[2][k].wait()
        loads[3][k].wait()
        sf[:, cols] = nn(act[2], vd[:, cols]) + vr[:, cols].astype(F32)
    pack(fb, sf, pf)
    po[:, 0:80, :] = pf[...].astype(BF)
    ahead = send(1, 0, 80)
    ahead.start()
    back.wait()
    ahead.wait()


def pack_selected(fb, bb, act, side, wg, wu, wd, res):
    whole = pl.BlockSpec(memory_space=pltpu.VMEM)
    smem = pl.BlockSpec(memory_space=pltpu.SMEM)
    anywhere = pl.BlockSpec(memory_space=pl.ANY)
    return pl.pallas_call(
        pack_kernel,
        in_specs=[smem] * 2 + [whole] * 2 + [anywhere] * 4,
        out_specs=anywhere,
        out_shape=pltpu.HBM((32, MSG, 128), BF),
        scratch_shapes=[pltpu.VMEM((F, D), BF)] * 3
        + [
            pltpu.VMEM((G, D), BF),
            pltpu.VMEM((G, D), F32),
            pltpu.VMEM((G, D), F32),
            pltpu.VMEM((32, 80, 128), F32),
            pltpu.VMEM((32, 80, 128), F32),
            pltpu.VMEM((32, MSG, 128), BF),
            pltpu.SemaphoreType.DMA((4 * CHUNKS + 2,)),
        ],
        compiler_params=pltpu.CompilerParams(vmem_limit_bytes=32 << 20),
        cost_estimate=pl.CostEstimate(
            flops=6 * G * F * D, bytes_accessed=2 * (G * D + 3 * F * D), transcendentals=0
        ),
        name="pack_selected",
    )(fb, bb, act, side, hbm(wg), hbm(wu), hbm(wd), hbm(res))


def residual_kernel(fb, fc, act, wd, res, res_next, sf):
    n = pl.program_id(0)
    nb = wd.shape[1]
    cols = pl.ds(pl.multiple_of(n * nb, nb), nb)
    sf[:, cols] = nn(act[0], wd[...]) + res[...].astype(F32)

    @pl.when(n == pl.num_programs(0) - 1)
    def _():
        def one(t, carry):
            r = pl.ds(pl.multiple_of(t * 8, 8), 8)
            count = fc[t]
            for j in range(KMAX):
                at = pl.ds(pl.multiple_of(fb[t, j] * 128, 128), 128)
                sf[r, at] = jnp.where(j < count, 0.0, sf[r, at])
            return carry

        lax.fori_loop(0, 32, one, 0)
        res_next[...] = sf[...].astype(BF)


def next_residual(fb, fc, act, wd, res):
    nb = 1280
    return pl.pallas_call(
        residual_kernel,
        grid_spec=pltpu.PrefetchScalarGridSpec(
            num_scalar_prefetch=2,
            grid=(D // nb,),
            in_specs=[
                pl.BlockSpec((1, G, F), lambda n, *_: (2, 0, 0)),
                pl.BlockSpec((F, nb), lambda n, *_: (0, n)),
                pl.BlockSpec((G, nb), lambda n, *_: (0, n)),
            ],
            out_specs=pl.BlockSpec((G, D), lambda n, *_: (0, 0)),
            scratch_shapes=[pltpu.VMEM((G, D), F32)],
        ),
        out_shape=jax.ShapeDtypeStruct((G, D), BF),
        compiler_params=pltpu.CompilerParams(vmem_limit_bytes=VMEM_LIMIT),
        cost_estimate=pl.CostEstimate(
            flops=2 * G * F * D, bytes_accessed=2 * (2 * G * D + F * D), transcendentals=0
        ),
        name="next_residual",
    )(fb, fc, act, wd, res)


def unpack_kernel(idx, data, of, ob, pk, *accs):
    pk[...] = data[...].astype(F32)
    for acc in accs:
        acc[...] = jnp.zeros_like(acc)

    def one(i, carry):
        for j in range(KMAX):
            for q in range(4):
                t = (q // 2) * 16 + i
                back = q % 2
                at = pl.ds(pl.multiple_of(idx[t, back * KMAX + j] * 128, 128), 128)
                row = pl.multiple_of(t * MSG + back * 80 + j * 8, 8)
                accs[q][:, at] += pk[pl.ds(row, 8), :]
        return carry

    lax.fori_loop(0, 16, one, 0)
    of[...] = (accs[0][:, :D] + accs[2][:, :D]).astype(BF)
    ob[...] = (accs[1][:, :D] + accs[3][:, :D]).astype(BF)


def unpack(idx, data):
    whole = pl.BlockSpec(memory_space=pltpu.VMEM)
    return pl.pallas_call(
        unpack_kernel,
        in_specs=[pl.BlockSpec(memory_space=pltpu.SMEM), whole],
        out_specs=[whole, whole],
        out_shape=[jax.ShapeDtypeStruct((8, D), BF)] * 2,
        scratch_shapes=[
            pltpu.VMEM((32 * MSG, 128), F32),
        ]
        + [pltpu.VMEM((8, D + 128), F32)] * 4,
        compiler_params=pltpu.CompilerParams(vmem_limit_bytes=12 << 20),
        cost_estimate=pl.CostEstimate(flops=10**6, bytes_accessed=2 * 10**6, transcendentals=0),
        name="unpack",
    )(idx, data)


def grads_kernel(core, act, *refs):
    far = refs[:16]
    og, ou, od, av, pv, acc, sem = refs[16:]
    copies = []
    for q in range(2):
        part = pl.ds(4 * q, 4)
        copies.append([pltpu.make_async_copy(act.at[part], av.at[part], sem.at[16 + q])])
        for i in (*range(4 * q, 4 * q + 4), *range(8 + 4 * q, 12 + 4 * q)):
            copies[-1].append(pltpu.make_async_copy(far[i], pv.at[i], sem.at[i]))
        for c in copies[-1]:
            c.start()

    def rows(first, s, n0, n1):
        blocks = []
        for i in range(4):
            for j in range(4):
                if s < 4:
                    blocks.append(pv[first + i, j, s, :, n0:n1])
                else:
                    blocks.append(pv[first + 4 + j, i, s - 4, :, n0:n1])
        return jnp.concatenate(blocks, axis=0)

    def run(q, tok, cot):
        for first, wanted in ((tok, ((0, og), (1, ou))), (cot, ((2, od),))):
            for n0, n1 in ((0, 256), (256, 512), (512, 640)):
                total = [None] * len(wanted)
                for s in range(4 * q, 4 * q + 4):
                    rhs = rows(first, s, n0, n1)
                    for w, (j, _) in enumerate(wanted):
                        term = nn(av[s, j], rhs)
                        total[w] = term if total[w] is None else total[w] + term
                for w, (j, out) in enumerate(wanted):
                    if q == 0:
                        acc[j, :, n0:n1] = total[w]
                    else:
                        out[:, n0:n1] = (acc[j, :, n0:n1] + total[w]).astype(BF)

    for q in range(2):
        for c in copies[q]:
            c.wait()

        @pl.when(core[0] == 0)
        def _():
            run(q, 0, 8)

        @pl.when(core[0] != 0)
        def _():
            run(q, 8, 0)


def grads(core, act, mine, other):
    whole = pl.BlockSpec(memory_space=pltpu.VMEM)
    return pl.pallas_call(
        grads_kernel,
        in_specs=[pl.BlockSpec(memory_space=pltpu.SMEM)] + [pl.BlockSpec(memory_space=pl.ANY)] * 17,
        out_specs=[whole] * 3,
        out_shape=[jax.ShapeDtypeStruct((F, 640), BF)] * 3,
        scratch_shapes=[
            pltpu.VMEM((8, 3, F, G), BF),
            pltpu.VMEM((16, 4, 4, 16, 640), BF),
            pltpu.VMEM((3, F, 640), F32),
            pltpu.SemaphoreType.DMA((18,)),
        ],
        compiler_params=pltpu.CompilerParams(vmem_limit_bytes=VMEM_LIMIT),
        cost_estimate=pl.CostEstimate(
            flops=6 * G * F * D, bytes_accessed=8 * 10**6, transcendentals=0
        ),
        name="grads",
    )(core, hbm(act), *[hbm(v) for v in (*mine, *other)])


def swap_core(v):
    return lax.ppermute(v, "core", [(0, 1), (1, 0)])


def shift(v, axis, size, by):
    return lax.ppermute(v, axis, [(i, (i + by) % size) for i in range(size)])


def shards(tok, wg, wu, wd, res, fb, fc, cot, bb, bc):
    core = lax.axis_index("core")
    which = core.astype(jnp.int32).reshape(1)
    fb, fc, bb, bc = fb[0, 0], fc[0, 0], bb[0, 0], bc[0, 0]

    rows = lax.all_gather(jnp.concatenate([tok, cot], axis=1), T, axis=0, tiled=True)

    blocks = [v.reshape(8, 8, 640).transpose(1, 0, 2) for v in (tok, cot)]
    blocks = jnp.stack(blocks, axis=1).reshape(16, 8, 640)
    cols = lax.all_to_all(blocks, ("dp", "core"), 0, 0, tiled=True).reshape(8, 16, 640)
    halves = [cols[:4], cols[4:]]
    steps = [shift(halves[h], a, 4, s) for s in (1, 3) for h, a in ((0, "x"), (1, "y"))]
    steps = [shift(steps[0], "x", 4, 1), shift(steps[1], "y", 4, 1), *steps]
    steps = lax.optimization_barrier(tuple(steps))
    four = [jnp.stack([halves[h], steps[2 + h], steps[h], steps[4 + h]]) for h in range(2)]
    slots = jnp.arange(KMAX)[None, :]
    lists = jnp.concatenate(
        [jnp.where(slots < fc[:, None], fb, 40), jnp.where(slots < bc[:, None], bb, 40)], axis=1
    )
    lists = jnp.broadcast_to(lists[:, None, :], (32, 16, 2 * KMAX))
    side = jnp.pad(lists, ((0, 0), (0, 0), (0, 128 - 2 * KMAX))).astype(F32)
    *four, side = lax.optimization_barrier((*four, side))
    mine = [four[0], None, None, None, four[1], None, None, None]
    for s in (1, 3):
        mine[s] = shift(four[0], "y", 4, s)
        mine[4 + s] = shift(four[1], "x", 4, s)
    mine[2], mine[6] = shift(mine[3], "y", 4, -1), shift(mine[7], "x", 4, -1)
    rows, *mine = lax.optimization_barrier((rows, *mine))

    where = jnp.stack([lax.axis_index("x"), lax.axis_index("y")]).astype(jnp.int32)
    nat, act = acts(where, rows, wg, wu, wd)
    everyone = lax.all_gather(act[None], "dp", axis=0, tiled=True)
    payload = pack_selected(fb, bb, nat, side, wg, wu, wd, res[0, 0])
    payload, nat, *mine = lax.optimization_barrier((payload, nat, *mine))
    received = lax.all_to_all(payload, T, 0, 0, tiled=True)
    others = [swap_core(v) for v in mine]
    nat, *others = lax.optimization_barrier((nat, *others))
    res_next = next_residual(fb, fc, nat, wd, res[0, 0])
    idx = received[:, 160, : 2 * KMAX].astype(jnp.int32)
    layer_output, input_gradient = unpack(idx, received.reshape(32 * MSG, 128))
    gate_gradient, up_gradient, down_gradient = grads(which, everyone, mine, others)
    return (
        layer_output,
        res_next[None, None],
        input_gradient,
        gate_gradient,
        up_gradient,
        down_gradient,
    )


def solution(mesh):
    fine = Mesh(mesh.devices.reshape(8, 4, 4, 2), ("dp", "x", "y", "core"))
    row = P(("dp",) + T, None)
    return jax.shard_map(
        shards,
        mesh=fine,
        in_specs=(
            row,
            P(T, None),
            P(T, None),
            P(T, None),
            P("dp", T, None, None),
            P("dp", T, None, None),
            P("dp", T, None),
            row,
            P("dp", T, None, None),
            P("dp", T, None),
        ),
        out_specs=(row, P("dp", T, None, None), row, P(T, "dp"), P(T, "dp"), P(T, "dp")),
        check_vma=False,
    )
```
